32 devices in a mesh: dp: 4 (over x, core), seq: 8 (over z, y).
Axes of the slice: x: 2, y: 2, z: 4, core: 2. Of those that a mesh axis runs over, the one named last changes fastest.
Arguments:
- pre_gate: bfloat16 [4, 1024, 2048], P('dp', 'seq'), may hold values from -6 to 6
- post_gate: bfloat16 [4, 1024, 2048], P('dp', 'seq'), may hold values from -6 to 6
- values: bfloat16 [4, 1024, 2048], P('dp', 'seq'), may hold values from -6 to 6
- cotangent: bfloat16 [4, 1024, 2048], P('dp', 'seq'), may hold values from -6 to 6
- filters: bfloat16 [1024, 16], P(('dp', 'seq')), may hold values from -0.1875 to 0.1875
Outputs:
- output: bfloat16 [4, 1024, 2048], P('dp', 'seq')
- grad_pre: bfloat16 [4, 1024, 2048], P('dp', 'seq')
- grad_post: bfloat16 [4, 1024, 2048], P('dp', 'seq')
- grad_values: bfloat16 [4, 1024, 2048], P('dp', 'seq')
- grad_filters: float32 [1024, 16], P(('dp', 'seq'))
The draws below stay inside these ranges and needn't reach their ends.
All inputs are finite; a program needn't handle non-finite values.
Results may differ from the reference program's by a relative error of at most 0.005.
Values may be sent and summed in bfloat16 or wider, within the bound.
No kernel may reach another device: no remote copies, remote signals or barrier semaphores. Data moves between devices by JAX's collectives and lax.ppermute only.
A program may use at most 128 MiB of HBM per device.

```python
import jax
import jax.numpy as jnp
from jax import lax

D = 2048
GS = 128
K = 1024
G = 16
SEQS = 4
LEN = 1024


def steps_of(own_key, dims, split, low, high):
    factor_of, own = 1.0, jax.random.fold_in(own_key, 6)
    for dim, blocks in split:
        heights = jnp.exp(jax.random.uniform(jax.random.fold_in(own, dim), (blocks,), jnp.float32, low / len(split), high / len(split)))
        factor_of = factor_of * jnp.repeat(heights, dims[dim] // blocks).reshape([-1 if axis == dim else 1 for axis in range(len(dims))])
    return factor_of


def scatter_about(stream_key, shape, deviation, most, cuts=(), dtype=jnp.bfloat16):
    values = deviation * jax.random.normal(stream_key, shape, jnp.float32)
    if cuts:
        values = values * steps_of(stream_key, shape, cuts, -0.22, 0.18)
    return jnp.clip(values, -most, most).astype(dtype)


def setup_inputs(seed: int = 0) -> dict:
    key_list = jax.random.split(jax.random.key(seed), 6)
    pre_gate = scatter_about(key_list[0], (SEQS, LEN, D), 1.0, 6.0, ((0, 4), (1, 8)))
    post_gate = scatter_about(key_list[1], (SEQS, LEN, D), 1.0, 6.0, ((0, 4), (1, 8)))
    values = scatter_about(key_list[2], (SEQS, LEN, D), 1.0, 6.0, ((0, 4), (1, 8)))
    cotangent = scatter_about(key_list[3], (SEQS, LEN, D), 1.0, 6.0, ((0, 4), (1, 8)))
    filters = scatter_about(key_list[4], (K, G), K ** -0.5, 0.1875, ((0, 32),))
    return {"pre_gate": pre_gate, "post_gate": post_gate, "values": values, "cotangent": cotangent, "filters": filters}


def reference(pre_gate, post_gate, values, cotangent, filters):
    length = LEN + K
    expanded = jnp.repeat(filters.astype(jnp.float32), GS, axis=1)
    spectrum = jnp.fft.rfft(expanded, n=length, axis=0)

    def one_sequence(items):
        pre_seq, post_seq, value_seq, cot_seq = items
        mixed_in = (pre_seq.astype(jnp.float32) * value_seq).astype(jnp.bfloat16)
        mixed_spec = jnp.fft.rfft(mixed_in.astype(jnp.float32), n=length, axis=0)
        convolved = jnp.fft.irfft(mixed_spec * spectrum, n=length, axis=0)[:LEN]
        output = (post_seq.astype(jnp.float32) * convolved).astype(jnp.bfloat16)
        grad_post = (cot_seq.astype(jnp.float32) * convolved).astype(jnp.bfloat16)
        gated = (cot_seq.astype(jnp.float32) * post_seq).astype(jnp.bfloat16)
        gated_spec = jnp.fft.rfft(gated.astype(jnp.float32), n=length, axis=0)
        carried = jnp.fft.irfft(gated_spec * jnp.conj(spectrum), n=length, axis=0)[:LEN]
        grad_pre = (carried * value_seq).astype(jnp.bfloat16)
        grad_values = (carried * pre_seq).astype(jnp.bfloat16)
        lagged = jnp.fft.irfft(gated_spec * jnp.conj(mixed_spec), n=length, axis=0)[:K]
        grouped = jnp.sum(lagged.reshape(K, G, GS), axis=2)
        return output, grad_pre, grad_post, grad_values, grouped

    output, grad_pre, grad_post, grad_values, grouped = lax.map(one_sequence, (pre_gate, post_gate, values, cotangent))
    grad_filters = jnp.sum(grouped, axis=0) / float((SEQS * LEN * GS) ** 0.5)
    return output, grad_pre, grad_post, grad_values, grad_filters
```

```python
import jax
import jax.numpy as jnp
import numpy as np
from jax import lax
from jax.experimental import pallas as pl
from jax.experimental.pallas import tpu as pltpu
from jax.sharding import PartitionSpec as P

K = 1024


def shifted(value, axis, steps):
    count = lax.axis_size(axis)
    first, last = (max(0, -steps), min(count, count - steps))
    return lax.ppermute(value, axis, [(source, source + steps) for source in range(first, last)])


def tile_index(lag_blocks, shard_len):
    offsets = np.arange(lag_blocks)[:, None, None] * shard_len
    rows_idx = np.arange(shard_len)[None, :, None]
    cols_idx = np.arange(shard_len)[None, None, :]
    return (offsets + rows_idx - cols_idx + shard_len).astype(np.int32)


def build_tiles(all_taps, lag_blocks, shard_len):
    tap_count = all_taps.shape[0]
    needed = (lag_blocks + 1) * shard_len
    trailing = max(needed - shard_len - tap_count, 0)
    padded = jnp.concatenate(
        [
            jnp.zeros((shard_len, all_taps.shape[1]), all_taps.dtype),
            all_taps,
            jnp.zeros((trailing, all_taps.shape[1]), all_taps.dtype),
        ],
        axis=0,
    )
    columns = padded.T
    return columns[:, tile_index(lag_blocks, shard_len)]


def earlier_relay(piece_in, history_len):

    def earlier_advance(moving, unused):
        arrived = shifted(moving, "seq", 1)
        return (arrived, arrived)

    unused_last, stacked = lax.scan(earlier_advance, piece_in, None, length=history_len)
    return jnp.concatenate([piece_in[None], stacked], axis=0)


def later_relay(piece_in, history_len):

    def later_advance(moving, unused):
        arrived = shifted(moving, "seq", -1)
        return (arrived, arrived)

    unused_last, stacked = lax.scan(later_advance, piece_in, None, length=history_len)
    return jnp.concatenate([piece_in[None], stacked], axis=0)


def lag_window(gated_rows, history, local_groups, group_width, lag_count):
    row_count = gated_rows.shape[0]
    span_len = history.shape[0]
    front_zero = jnp.zeros((row_count, history.shape[1]), history.dtype)
    widened = jnp.concatenate([front_zero, history], axis=0)
    gated_grp = gated_rows.reshape(row_count, local_groups, group_width).transpose(1, 0, 2)
    hist_grp = widened.reshape(span_len + row_count, local_groups, group_width).transpose(1, 0, 2)

    def one_group(pair_in):
        gated_one, hist_one = pair_in
        product = lax.dot_general(
            gated_one, hist_one, (((1,), (1,)), ((), ())), preferred_element_type=jnp.float32
        )
        padded = jnp.pad(product, ((0, 0), (0, row_count)))
        flat_line = jnp.concatenate(
            [padded.reshape(-1), jnp.zeros((row_count,), jnp.float32)], axis=0
        )
        skewed = flat_line.reshape(row_count, span_len + 2 * row_count + 1)
        diag_sums = jnp.sum(skewed, axis=0)
        return jnp.flip(diag_sums[1 : span_len + 1], axis=0)[:lag_count]

    return lax.map(one_group, (gated_grp, hist_grp))


def shards(pre_gate, post_gate, values, cotangent, filters):
    shard_len = pre_gate.shape[1]
    channels = pre_gate.shape[2]
    groups = filters.shape[1]
    group_size = channels // groups
    seq_count = lax.axis_size("seq")
    all_taps = lax.all_gather(filters, ("dp", "seq"), axis=0, tiled=True)
    mixed_in = (pre_gate[0].astype(jnp.float32) * values[0]).astype(jnp.bfloat16)
    gated = (cotangent[0].astype(jnp.float32) * post_gate[0]).astype(jnp.bfloat16)
    history_len = min(-(-K // shard_len), seq_count - 1)
    lag_blocks = history_len + 1
    mixed_ext = earlier_relay(mixed_in, history_len)
    gated_ext = later_relay(gated, history_len)
    mixed_four = mixed_ext.reshape(lag_blocks, shard_len, groups, group_size)
    gated_four = gated_ext.reshape(lag_blocks, shard_len, groups, group_size)
    tiles = build_tiles(all_taps, lag_blocks, shard_len)
    convolved = jnp.einsum(
        "gmij,mjgc->igc", tiles, mixed_four, preferred_element_type=jnp.float32
    ).reshape(shard_len, channels)
    carried = jnp.einsum(
        "gmji,mjgc->igc", tiles, gated_four, preferred_element_type=jnp.float32
    ).reshape(shard_len, channels)
    hist_len = lag_blocks * shard_len
    lag_count = min(K, hist_len)
    history = jnp.flip(mixed_ext, axis=0).reshape(hist_len, channels)
    lag_local = lag_window(gated, history, groups, group_size, lag_count)
    partial_grads = lag_local.T
    output = (post_gate[0].astype(jnp.float32) * convolved).astype(jnp.bfloat16)
    grad_post = (cotangent[0].astype(jnp.float32) * convolved).astype(jnp.bfloat16)
    grad_pre = (carried * values[0]).astype(jnp.bfloat16)
    grad_values = (carried * pre_gate[0]).astype(jnp.bfloat16)
    owned = lax.psum_scatter(partial_grads, ("dp", "seq"), scatter_dimension=0, tiled=True)
    total_tokens = lax.axis_size("dp") * shard_len * seq_count * group_size
    grad_filters = owned / float(total_tokens**0.5)
    return (output[None], grad_pre[None], grad_post[None], grad_values[None], grad_filters)


BLOCK = 128


def swap_fits(pre_gate, post_gate, values, cotangent, filters):
    seq_count, dp_count = lax.axis_size("seq"), lax.axis_size("dp")
    channels, groups = pre_gate.shape[2], filters.shape[1]
    return (
        groups % seq_count == 0
        and channels // groups == BLOCK
        and pre_gate.shape[0] == 1
        and pre_gate.shape[1] == BLOCK
        and seq_count % 2 == 0
        and seq_count & (seq_count - 1) == 0
        and seq_count * BLOCK == K
        and filters.shape[0] * seq_count * dp_count == K
    )


def pack_kernel(pre_ref, post_ref, values_ref, cot_ref, out_ref):
    f32 = jnp.float32
    out_ref[0, :BLOCK] = (pre_ref[0].astype(f32) * values_ref[0].astype(f32)).astype(jnp.bfloat16)
    out_ref[0, BLOCK:] = (cot_ref[0].astype(f32) * post_ref[0].astype(f32)).astype(jnp.bfloat16)


def gate_and_pack(pre_gate, post_gate, values, cotangent, parts):
    width = pre_gate.shape[2] // parts
    spec = pl.BlockSpec((1, BLOCK, width), lambda i: (0, 0, i))
    return pl.pallas_call(
        pack_kernel,
        grid=(parts,),
        in_specs=[spec] * 4,
        out_specs=pl.BlockSpec((1, 2 * BLOCK, width), lambda i: (i, 0, 0)),
        out_shape=jax.ShapeDtypeStruct((parts, 2 * BLOCK, width), jnp.bfloat16),
        cost_estimate=pl.CostEstimate(flops=4 * pre_gate.size, bytes_accessed=12 * pre_gate.size, transcendentals=0),
        name="gate_and_pack",
    )(pre_gate, post_gate, values, cotangent)


def toeplitz_kernel(parts, dp_count, rows, index_ref, *refs):
    pieces, (causal_ref, anti_ref, taps_ref) = refs[:parts], refs[parts:]
    dp_index, seq_index = index_ref[0], index_ref[1]
    for q in range(parts):
        source = lax.rem(seq_index + parts - q, parts)
        piece = pieces[q][...].astype(jnp.float32)
        for p in range(dp_count):
            owner = lax.rem(dp_index + dp_count - p, dp_count)
            taps_ref[owner * parts + source] = piece[:, p * rows : (p + 1) * rows]
    local = causal_ref.shape[0]
    for g in range(local):
        which = pl.ds(seq_index * local + g, 1)
        line = jnp.concatenate([taps_ref[o, which, :] for o in range(parts * dp_count)], axis=1)
        line = jnp.concatenate([line, jnp.zeros((1, 2 * BLOCK), jnp.float32)], axis=1)
        spread = jnp.broadcast_to(line, (2 * BLOCK, K + 2 * BLOCK))
        shear = pltpu.roll(spread, 0, 1, stride=1, stride_axis=0)
        anti_ref[g] = shear[:, :K].astype(jnp.bfloat16)
        count = K // BLOCK
        turned = [shear[:BLOCK, m * BLOCK : (m + 1) * BLOCK].T.astype(jnp.bfloat16) for m in range(count)]
        turned.append(jnp.zeros((BLOCK, BLOCK), jnp.bfloat16))
        for b in range(count):
            causal_ref[g, :BLOCK, b * BLOCK : (b + 1) * BLOCK] = turned[count - 2 - b]
            causal_ref[g, BLOCK:, b * BLOCK : (b + 1) * BLOCK] = turned[count - 1 - b]


def toeplitz(filters):
    parts, dp_count = lax.axis_size("seq"), lax.axis_size("dp")
    dp_index, seq_index = lax.axis_index("dp"), lax.axis_index("seq")
    rows, groups = filters.shape
    local = groups // parts
    own = filters.T
    along = [own]
    for p in range(1, dp_count):
        along.append(lax.ppermute(own, "dp", [(i, (i + p) % dp_count) for i in range(dp_count)]))
    own = jnp.concatenate(along, axis=1)
    pieces = [own]
    for q in range(1, parts):
        pieces.append(lax.ppermute(own, "seq", [(i, (i + q) % parts) for i in range(parts)]))
    band = jax.ShapeDtypeStruct((local, 2 * BLOCK, K), jnp.bfloat16)
    vmem = pl.BlockSpec(memory_space=pltpu.VMEM)
    return pl.pallas_call(
        lambda *refs: toeplitz_kernel(parts, dp_count, rows, *refs),
        in_specs=[pl.BlockSpec(memory_space=pltpu.SMEM)] + [vmem] * parts,
        out_specs=[vmem, vmem],
        out_shape=[band, band],
        scratch_shapes=[pltpu.VMEM((parts * dp_count, groups, rows), jnp.float32)],
        cost_estimate=pl.CostEstimate(flops=2_000_000, bytes_accessed=2_000_000, transcendentals=0),
        name="toeplitz",
    )(jnp.stack([dp_index, seq_index]).astype(jnp.int32), *pieces)


def convolve_kernel(slabs_ref, causal_ref, anti_ref, out_ref):
    blocks, _, width = slabs_ref.shape
    length = blocks * BLOCK
    for g in range(width // BLOCK):
        lanes = slice(g * BLOCK, (g + 1) * BLOCK)
        mixed = slabs_ref[:, :BLOCK, lanes].reshape(length, BLOCK)
        gated = slabs_ref[:, BLOCK:, lanes].reshape(length, BLOCK)
        for p in range(blocks // 2):
            reach = (p + 1) * 2 * BLOCK
            ahead = length - p * 2 * BLOCK
            convolved = jnp.dot(causal_ref[g, :, K - reach :], mixed[:reach], preferred_element_type=jnp.float32)
            carried = jnp.dot(anti_ref[g, :, :ahead], gated[length - ahead :], preferred_element_type=jnp.float32)
            pair = slice(2 * p, 2 * p + 2)
            out_ref[pair, :BLOCK, lanes] = convolved.reshape(2, BLOCK, BLOCK).astype(jnp.bfloat16)
            out_ref[pair, BLOCK:, lanes] = carried.reshape(2, BLOCK, BLOCK).astype(jnp.bfloat16)


def convolve(slabs, causal, anti):
    vmem = pl.BlockSpec(memory_space=pltpu.VMEM)
    return pl.pallas_call(
        convolve_kernel,
        in_specs=[vmem] * 3,
        out_specs=vmem,
        out_shape=jax.ShapeDtypeStruct(slabs.shape, jnp.bfloat16),
        cost_estimate=pl.CostEstimate(flops=1_300_000_000, bytes_accessed=4 * slabs.size, transcendentals=0),
        name="convolve",
    )(slabs, causal, anti)


def lag_kernel(slabs_ref, out_ref):
    blocks, _, width = slabs_ref.shape
    length = blocks * BLOCK
    count = length + BLOCK
    exchange = (
        lax.broadcasted_iota(jnp.int32, (BLOCK, BLOCK), 0) + lax.broadcasted_iota(jnp.int32, (BLOCK, BLOCK), 1)
        == BLOCK - 1
    ).astype(jnp.bfloat16)
    turned = [
        jnp.dot(exchange, slabs_ref[j, :BLOCK, :], preferred_element_type=jnp.float32).astype(jnp.bfloat16)
        for j in range(blocks)
    ]
    for g in range(width // BLOCK):
        lanes = slice(g * BLOCK, (g + 1) * BLOCK)
        mixed = jnp.concatenate([block[:, lanes] for block in turned], axis=0)
        sums = [None] * blocks
        for i in range(blocks):
            gated = slabs_ref[i, BLOCK:, lanes]
            product = lax.dot_general(
                mixed[: (i + 1) * BLOCK], gated, (((1,), (1,)), ((), ())), preferred_element_type=jnp.float32
            )
            for j in range(i + 1):
                term = product[j * BLOCK : (j + 1) * BLOCK]
                sums[i - j] = term if sums[i - j] is None else sums[i - j] + term
        table = jnp.concatenate(sums + [jnp.zeros((BLOCK, BLOCK), jnp.float32)], axis=1)
        shear = pltpu.roll(table, 0, 1, stride=1, stride_axis=0)
        line = pltpu.roll(jnp.sum(shear, axis=0, keepdims=True), count - BLOCK + 1, 1)[:, :length]
        span = length // out_ref.shape[0]
        for d in range(out_ref.shape[0]):
            out_ref[d, g : g + 1] = line[:, d * span : (d + 1) * span]


def lag_sums(slabs, dp_count):
    blocks, _, width = slabs.shape
    vmem = pl.BlockSpec(memory_space=pltpu.VMEM)
    return pl.pallas_call(
        lag_kernel,
        in_specs=[vmem],
        out_specs=vmem,
        out_shape=jax.ShapeDtypeStruct((dp_count, width // BLOCK, K // dp_count), jnp.float32),
        cost_estimate=pl.CostEstimate(flops=600_000_000, bytes_accessed=2 * slabs.size, transcendentals=0),
        name="lag_sums",
    )(slabs)


def owned_lags(shares):
    dp_count, local, span = shares.shape
    parts = lax.axis_size("seq")
    dp_index, seq_index = lax.axis_index("dp"), lax.axis_index("seq")
    total = lax.dynamic_index_in_dim(shares, dp_index, 0, keepdims=False)
    for p in range(1, dp_count):
        share = lax.dynamic_index_in_dim(shares, lax.rem(dp_index + p, dp_count), 0, keepdims=False)
        total = total + lax.ppermute(share, "dp", [(i, (i + p) % dp_count) for i in range(dp_count)])
    step = 1
    while step < parts:
        other = lax.ppermute(total, "seq", [(i, i ^ step) for i in range(parts)])
        upper = (seq_index // step) % 2 == 1
        total = jnp.where(upper, jnp.concatenate([other, total]), jnp.concatenate([total, other]))
        step *= 2
    rows = span // parts
    return lax.dynamic_slice_in_dim(total, seq_index * rows, rows, 1)


def gates_kernel(pre_ref, post_ref, values_ref, cot_ref, back_ref, out_ref, pre_out, post_out, values_out):
    f32, bf16 = jnp.float32, jnp.bfloat16
    convolved, carried = back_ref[0, :BLOCK].astype(f32), back_ref[0, BLOCK:].astype(f32)
    out_ref[0] = (post_ref[0].astype(f32) * convolved).astype(bf16)
    post_out[0] = (cot_ref[0].astype(f32) * convolved).astype(bf16)
    pre_out[0] = (carried * values_ref[0].astype(f32)).astype(bf16)
    values_out[0] = (carried * pre_ref[0].astype(f32)).astype(bf16)


def gate_outputs(pre_gate, post_gate, values, cotangent, back):
    parts, _, width = back.shape
    spec = pl.BlockSpec((1, BLOCK, width), lambda i: (0, 0, i))
    shape = jax.ShapeDtypeStruct(pre_gate.shape, jnp.bfloat16)
    return pl.pallas_call(
        gates_kernel,
        grid=(parts,),
        in_specs=[spec] * 4 + [pl.BlockSpec((1, 2 * BLOCK, width), lambda i: (i, 0, 0))],
        out_specs=[spec] * 4,
        out_shape=[shape] * 4,
        cost_estimate=pl.CostEstimate(flops=4 * pre_gate.size, bytes_accessed=20 * pre_gate.size, transcendentals=0),
        name="gate_outputs",
    )(pre_gate, post_gate, values, cotangent, back)


def swapped(pre_gate, post_gate, values, cotangent, filters):
    parts, dp_count = lax.axis_size("seq"), lax.axis_size("dp")
    packed = gate_and_pack(pre_gate, post_gate, values, cotangent, parts)
    slabs = lax.all_to_all(packed, "seq", 0, 0, tiled=True)
    causal, anti = toeplitz(filters)
    back = lax.all_to_all(convolve(slabs, causal, anti), "seq", 0, 0, tiled=True)
    output, grad_pre, grad_post, grad_values = gate_outputs(pre_gate, post_gate, values, cotangent, back)
    total_tokens = dp_count * parts * pre_gate.shape[1] * (pre_gate.shape[2] // filters.shape[1])
    grad_filters = owned_lags(lag_sums(slabs, dp_count)).T / float(total_tokens**0.5)
    return output, grad_pre, grad_post, grad_values, grad_filters


def solution(mesh):
    def chosen(*shard):
        fits = swap_fits(*shard)
        return (swapped if fits else shards)(*shard)

    return jax.shard_map(
        chosen,
        mesh=mesh,
        in_specs=(
            P("dp", "seq", None),
            P("dp", "seq", None),
            P("dp", "seq", None),
            P("dp", "seq", None),
            P(("dp", "seq"), None),
        ),
        out_specs=(
            P("dp", "seq", None),
            P("dp", "seq", None),
            P("dp", "seq", None),
            P("dp", "seq", None),
            P(("dp", "seq"), None),
        ),
        check_vma=False,
    )
```

```python
import jax
import jax.numpy as jnp
import numpy as np
from jax import lax
from jax.experimental import pallas as pl
from jax.experimental.pallas import tpu as pltpu
from jax.sharding import PartitionSpec as P

K = 1024


def shifted(value, axis, steps):
    count = lax.axis_size(axis)
    first, last = (max(0, -steps), min(count, count - steps))
    return lax.ppermute(value, axis, [(source, source + steps) for source in range(first, last)])


def tile_index(lag_blocks, shard_len):
    offsets = np.arange(lag_blocks)[:, None, None] * shard_len
    rows_idx = np.arange(shard_len)[None, :, None]
    cols_idx = np.arange(shard_len)[None, None, :]
    return (offsets + rows_idx - cols_idx + shard_len).astype(np.int32)


def build_tiles(all_taps, lag_blocks, shard_len):
    tap_count = all_taps.shape[0]
    needed = (lag_blocks + 1) * shard_len
    trailing = max(needed - shard_len - tap_count, 0)
    padded = jnp.concatenate(
        [
            jnp.zeros((shard_len, all_taps.shape[1]), all_taps.dtype),
            all_taps,
            jnp.zeros((trailing, all_taps.shape[1]), all_taps.dtype),
        ],
        axis=0,
    )
    columns = padded.T
    return columns[:, tile_index(lag_blocks, shard_len)]


def earlier_relay(piece_in, history_len):

    def earlier_advance(moving, unused):
        arrived = shifted(moving, "seq", 1)
        return (arrived, arrived)

    unused_last, stacked = lax.scan(earlier_advance, piece_in, None, length=history_len)
    return jnp.concatenate([piece_in[None], stacked], axis=0)


def later_relay(piece_in, history_len):

    def later_advance(moving, unused):
        arrived = shifted(moving, "seq", -1)
        return (arrived, arrived)

    unused_last, stacked = lax.scan(later_advance, piece_in, None, length=history_len)
    return jnp.concatenate([piece_in[None], stacked], axis=0)


def lag_window(gated_rows, history, local_groups, group_width, lag_count):
    row_count = gated_rows.shape[0]
    span_len = history.shape[0]
    front_zero = jnp.zeros((row_count, history.shape[1]), history.dtype)
    widened = jnp.concatenate([front_zero, history], axis=0)
    gated_grp = gated_rows.reshape(row_count, local_groups, group_width).transpose(1, 0, 2)
    hist_grp = widened.reshape(span_len + row_count, local_groups, group_width).transpose(1, 0, 2)

    def one_group(pair_in):
        gated_one, hist_one = pair_in
        product = lax.dot_general(
            gated_one, hist_one, (((1,), (1,)), ((), ())), preferred_element_type=jnp.float32
        )
        padded = jnp.pad(product, ((0, 0), (0, row_count)))
        flat_line = jnp.concatenate(
            [padded.reshape(-1), jnp.zeros((row_count,), jnp.float32)], axis=0
        )
        skewed = flat_line.reshape(row_count, span_len + 2 * row_count + 1)
        diag_sums = jnp.sum(skewed, axis=0)
        return jnp.flip(diag_sums[1 : span_len + 1], axis=0)[:lag_count]

    return lax.map(one_group, (gated_grp, hist_grp))


def shards(pre_gate, post_gate, values, cotangent, filters):
    shard_len = pre_gate.shape[1]
    channels = pre_gate.shape[2]
    groups = filters.shape[1]
    group_size = channels // groups
    seq_count = lax.axis_size("seq")
    all_taps = lax.all_gather(filters, ("dp", "seq"), axis=0, tiled=True)
    mixed_in = (pre_gate[0].astype(jnp.float32) * values[0]).astype(jnp.bfloat16)
    gated = (cotangent[0].astype(jnp.float32) * post_gate[0]).astype(jnp.bfloat16)
    history_len = min(-(-K // shard_len), seq_count - 1)
    lag_blocks = history_len + 1
    mixed_ext = earlier_relay(mixed_in, history_len)
    gated_ext = later_relay(gated, history_len)
    mixed_four = mixed_ext.reshape(lag_blocks, shard_len, groups, group_size)
    gated_four = gated_ext.reshape(lag_blocks, shard_len, groups, group_size)
    tiles = build_tiles(all_taps, lag_blocks, shard_len)
    convolved = jnp.einsum(
        "gmij,mjgc->igc", tiles, mixed_four, preferred_element_type=jnp.float32
    ).reshape(shard_len, channels)
    carried = jnp.einsum(
        "gmji,mjgc->igc", tiles, gated_four, preferred_element_type=jnp.float32
    ).reshape(shard_len, channels)
    hist_len = lag_blocks * shard_len
    lag_count = min(K, hist_len)
    history = jnp.flip(mixed_ext, axis=0).reshape(hist_len, channels)
    lag_local = lag_window(gated, history, groups, group_size, lag_count)
    partial_grads = lag_local.T
    output = (post_gate[0].astype(jnp.float32) * convolved).astype(jnp.bfloat16)
    grad_post = (cotangent[0].astype(jnp.float32) * convolved).astype(jnp.bfloat16)
    grad_pre = (carried * values[0]).astype(jnp.bfloat16)
    grad_values = (carried * pre_gate[0]).astype(jnp.bfloat16)
    owned = lax.psum_scatter(partial_grads, ("dp", "seq"), scatter_dimension=0, tiled=True)
    total_tokens = lax.axis_size("dp") * shard_len * seq_count * group_size
    grad_filters = owned / float(total_tokens**0.5)
    return (output[None], grad_pre[None], grad_post[None], grad_values[None], grad_filters)


BLOCK = 128


def swap_fits(pre_gate, post_gate, values, cotangent, filters):
    parts, dp_count = lax.axis_size("seq"), lax.axis_size("dp")
    channels, groups = pre_gate.shape[2], filters.shape[1]
    return (
        parts >= 4
        and parts & (parts - 1) == 0
        and groups % parts == 0
        and channels // groups == BLOCK
        and pre_gate.shape[0] == 1
        and pre_gate.shape[1] == BLOCK
        and parts * BLOCK == K
        and filters.shape[0] * parts * dp_count == K
    )


def swap(chunk, flip):
    count = lax.axis_size("seq")
    return lax.ppermute(chunk, "seq", [(i, i ^ flip) for i in range(count)])


def vmem_specs(count):
    return [pl.BlockSpec(memory_space=pltpu.VMEM)] * count


def chunk_shapes(count, width, blocks=1):
    return [jax.ShapeDtypeStruct((blocks * BLOCK, width), jnp.bfloat16)] * count


def call(kernel, name, place, operands, out_shape, scratch=(), flops=1000, nbytes=1000, after=()):
    def body(place_ref, *refs):
        kernel(place_ref, *refs[: len(operands)], *refs[len(operands) + len(after) :])

    return pl.pallas_call(
        body,
        in_specs=[pl.BlockSpec(memory_space=pltpu.SMEM)]
        + vmem_specs(len(operands))
        + [pl.BlockSpec(memory_space=pl.ANY)] * len(after),
        out_specs=vmem_specs(len(out_shape)),
        out_shape=out_shape,
        scratch_shapes=list(scratch),
        compiler_params=pltpu.CompilerParams(vmem_limit_bytes=20 * 1024 * 1024),
        cost_estimate=pl.CostEstimate(flops=flops, bytes_accessed=nbytes, transcendentals=0),
        name=name,
    )(place, *operands, *after)


TAIL = 16


def pack_kernel(quarters, pieces, place_ref, *refs):
    f32, bf16 = jnp.float32, jnp.bfloat16
    taps_in, (a_ref, b_ref), refs = refs[:pieces], refs[pieces : pieces + 2], refs[pieces + 2 :]
    a_outs, outs, (taps_ref,) = refs[:quarters], refs[quarters : 2 * quarters], refs[2 * quarters :]
    quarter = place_ref[1]
    width = a_outs[0].shape[1]
    local = taps_ref.shape[1]
    taps = jnp.concatenate([piece[...].astype(f32) for piece in taps_in], axis=1)
    for i in range(quarters):
        taps_ref[i] = taps[i * local : (i + 1) * local]
    for j in range(quarters):
        columns = pl.ds(pl.multiple_of((quarter ^ j) * width, width), width)
        a = a_ref[:, columns]
        a_outs[j][...] = a
        outs[j][:BLOCK] = a
        outs[j][BLOCK : 2 * BLOCK] = b_ref[:, columns]
        outs[j][2 * BLOCK :] = jnp.zeros((TAIL, width), bf16)
        taps = taps_ref[quarter ^ j]
        taps = jnp.concatenate([taps, jnp.zeros((TAIL - local, BLOCK), f32)], axis=0)
        outs[j][2 * BLOCK :, :BLOCK] = taps.astype(bf16)


def bands(quarters, dp_count, place_ref, taps_in, taps_ref, causal_ref, anti_ref):
    half, quarter, dp_index = place_ref[0], place_ref[1], place_ref[2]
    local, rows = taps_ref.shape[1:]
    for u in range(2):
        piece = taps_in[u][...].astype(jnp.float32)
        for j in range(quarters):
            for p in range(dp_count):
                owner = lax.rem(dp_index + dp_count - p, dp_count) * 2 * quarters + (half ^ u) * quarters + (quarter ^ j)
                start = j * BLOCK + p * rows
                taps_ref[owner] = piece[:local, start : start + rows]
    for g in range(local):
        line = jnp.concatenate([taps_ref[o, g : g + 1] for o in range(taps_ref.shape[0])], axis=1)
        line = jnp.concatenate([line, jnp.zeros((1, 2 * BLOCK), jnp.float32)], axis=1)
        spread = jnp.broadcast_to(line, (2 * BLOCK, K + 2 * BLOCK))
        shear = pltpu.roll(spread, 0, 1, stride=1, stride_axis=0)
        anti_ref[g] = shear[:, :K].astype(jnp.bfloat16)
        count = K // BLOCK
        turned = [shear[:BLOCK, m * BLOCK : (m + 1) * BLOCK].T.astype(jnp.bfloat16) for m in range(count)]
        turned.append(jnp.zeros((BLOCK, BLOCK), jnp.bfloat16))
        for b in range(count):
            causal_ref[g, :BLOCK, b * BLOCK : (b + 1) * BLOCK] = turned[count - 2 - b]
            causal_ref[g, BLOCK:, b * BLOCK : (b + 1) * BLOCK] = turned[count - 1 - b]


def in_order(scratch_ref, quarter, chunks):
    for j, chunk in enumerate(chunks):
        scratch_ref[quarter ^ j] = chunk[...]


def rows_of(ref, lanes):
    return ref[:, :, lanes].reshape(ref.shape[0] * BLOCK, BLOCK)


def dot(left, right):
    return jnp.dot(left, right, preferred_element_type=jnp.float32)


def causal_part(band, data, p):
    reach = (p + 1) * 2 * BLOCK
    return dot(band[:, K - reach :], data[:reach])


def anti_part(band, data, p):
    return dot(band[:, : data.shape[0] - p * 2 * BLOCK], data[p * 2 * BLOCK :])


def lag_lines(mixed, gated, first, turn):
    count = mixed.shape[0] // BLOCK
    blocks = K // BLOCK
    turned = jnp.concatenate(
        [dot(turn, mixed[j * BLOCK : (j + 1) * BLOCK]).astype(jnp.bfloat16) for j in range(count)], axis=0
    )
    sums = [None] * blocks
    for i in range(count):
        top = min(count, first + i + 1)
        product = lax.dot_general(
            turned[: top * BLOCK],
            gated[i * BLOCK : (i + 1) * BLOCK],
            (((1,), (1,)), ((), ())),
            preferred_element_type=jnp.float32,
        )
        for j in range(top):
            term = product[j * BLOCK : (j + 1) * BLOCK]
            lag = first + i - j
            sums[lag] = term if sums[lag] is None else sums[lag] + term
    last = max(m for m in range(blocks) if sums[m] is not None)
    zero = jnp.zeros((BLOCK, BLOCK), jnp.float32)
    table = jnp.concatenate([zero if t is None else t for t in sums[: last + 1]] + [zero], axis=1)
    span = (last + 2) * BLOCK
    shear = jnp.sum(pltpu.roll(table, 0, 1, stride=1, stride_axis=0), axis=0, keepdims=True)
    if span < K:
        shear = jnp.concatenate([shear, jnp.zeros((1, K + BLOCK - span), jnp.float32)], axis=1)
    return pltpu.roll(shear, K + BLOCK - (BLOCK - 1), 1)[:, :K]


def exchange():
    rows = lax.broadcasted_iota(jnp.int32, (BLOCK, BLOCK), 0)
    columns = lax.broadcasted_iota(jnp.int32, (BLOCK, BLOCK), 1)
    return jnp.where(rows + columns == BLOCK - 1, 1.0, 0.0).astype(jnp.bfloat16)


def local_kernel(quarters, dp_count, place_ref, *refs):
    taps_in, refs = refs[:2], refs[2:]
    ab_in, a_out = refs[:quarters], refs[quarters : 2 * quarters]
    causal_ref, anti_ref, sums_ref, lines_ref, a_ref, b_ref, done_ref, taps_ref = refs[2 * quarters :]
    bands(quarters, dp_count, place_ref, taps_in, taps_ref, causal_ref, anti_ref)
    half, quarter = place_ref[0], place_ref[1]
    in_order(a_ref, quarter, [ab.at[:BLOCK] for ab in ab_in])
    in_order(b_ref, quarter, [ab.at[BLOCK : 2 * BLOCK] for ab in ab_in])
    turn = exchange()

    def work(a_band, a_part, b_band, b_part, a_mixed):
        for g in range(causal_ref.shape[0]):
            lanes = slice(g * BLOCK, (g + 1) * BLOCK)
            a_rows, b_rows = rows_of(a_ref, lanes), rows_of(b_ref, lanes)
            for p in range(quarters // 2):
                pair = slice(2 * p, 2 * p + 2)
                a_sum = a_part(a_band.at[g], a_rows, p).reshape(2, BLOCK, BLOCK)
                done_ref[pair, :, lanes] = a_sum.astype(jnp.bfloat16)
                sums_ref[pair, :, lanes] = b_part(b_band.at[g], b_rows, p).reshape(2, BLOCK, BLOCK)
            mixed, gated = (a_rows, b_rows) if a_mixed else (b_rows, a_rows)
            lines_ref[g : g + 1] = lag_lines(mixed, gated, 0, turn)

    @pl.when(half == 0)
    def lower():
        work(causal_ref, causal_part, anti_ref, anti_part, True)

    @pl.when(half != 0)
    def upper():
        work(anti_ref, anti_part, causal_ref, causal_part, False)

    for j in range(quarters):
        a_out[j][...] = done_ref[quarter ^ j]


def lag_kernel(quarters, place_ref, *refs):
    a_in, r_in = refs[:quarters], refs[quarters : 2 * quarters]
    lines_ref, out_ref, mixed_ref, gated_ref, total_ref = refs[2 * quarters :]
    half, quarter = place_ref[0], place_ref[1]
    width = mixed_ref.shape[2]
    count = width // BLOCK
    turn = exchange()

    def gather(mixed, gated, lanes):
        for j in range(quarters):
            mixed_ref[quarter ^ j] = mixed[j][:BLOCK, lanes]
            gated_ref[quarter ^ j] = gated[j][:BLOCK, lanes]

    @pl.when(half == 0)
    def lower():
        gather(a_in, r_in, slice(0, width))

    @pl.when(half != 0)
    def upper():
        gather(r_in, a_in, slice(width, 2 * width))

    total_ref[...] = lines_ref[...]
    cross = []
    for g in range(count):
        lanes = slice(g * BLOCK, (g + 1) * BLOCK)
        cross.append(lag_lines(rows_of(mixed_ref, lanes), rows_of(gated_ref, lanes), quarters, turn))
    cross = jnp.concatenate(cross, axis=0)

    @pl.when(half == 0)
    def add_lower():
        total_ref[:count] += cross

    @pl.when(half != 0)
    def add_upper():
        total_ref[count:] += cross

    owners, step = out_ref.shape[0], K // out_ref.shape[0]
    for o in range(owners):
        start = o * step // BLOCK * BLOCK
        out_ref[o] = total_ref[:, start : start + BLOCK]


def cross_kernel(quarters, place_ref, *refs):
    ab_in, r_in = refs[:quarters], refs[quarters : 2 * quarters]
    lines_ref, sums_ref, causal_ref, anti_ref, shares_ref = refs[2 * quarters : 2 * quarters + 5]
    b_out = refs[2 * quarters + 5 : 3 * quarters + 5]
    r_ref, done_ref, mixed_ref, gated_ref, total_ref = refs[3 * quarters + 5 :]
    lag_kernel(quarters, place_ref, *ab_in, *r_in, lines_ref, shares_ref, mixed_ref, gated_ref, total_ref)
    half, quarter = place_ref[0], place_ref[1]
    in_order(r_ref, quarter, r_in)
    length = quarters * BLOCK

    def work(band, first):
        for g in range(causal_ref.shape[0]):
            lanes = slice(g * BLOCK, (g + 1) * BLOCK)
            rows = rows_of(r_ref, lanes)
            for p in range(quarters // 2):
                pair = slice(2 * p, 2 * p + 2)
                start = first(p * 2 * BLOCK)
                part = dot(band[g, :, start : start + length], rows).reshape(2, BLOCK, BLOCK)
                done_ref[pair, :, lanes] = (sums_ref[pair, :, lanes] + part).astype(jnp.bfloat16)

    @pl.when(half == 0)
    def lower():
        work(anti_ref, lambda row: length - row)

    @pl.when(half != 0)
    def upper():
        work(causal_ref, lambda row: K - length - row - 2 * BLOCK)

    for j in range(quarters):
        b_out[j][...] = done_ref[quarter ^ j]


def outputs_kernel(quarters, place_ref, *refs):
    f32, bf16 = jnp.float32, jnp.bfloat16
    a_in, b_in, refs = refs[:quarters], refs[quarters : 2 * quarters], refs[2 * quarters :]
    inputs, outputs, stores, results, (in_sem, out_sem) = refs[:4], refs[4:8], refs[8:12], refs[12:16], refs[16:]
    half, quarter = place_ref[0], place_ref[1]
    width = a_in[0].shape[1]

    def copies(j, out):
        columns = pl.ds(pl.multiple_of((quarter ^ j) * width, width), width)
        if out:
            return [
                pltpu.make_async_copy(store.at[j], target.at[0, :, columns], out_sem.at[j, i])
                for i, (store, target) in enumerate(zip(results, outputs))
            ]
        return [
            pltpu.make_async_copy(source.at[0, :, columns], store.at[j], in_sem.at[j, i])
            for i, (source, store) in enumerate(zip(inputs, stores))
        ]

    for j in range(quarters):
        for copy in copies(j, False):
            copy.start()
    for j in range(quarters):
        for copy in copies(j, False):
            copy.wait()
        pre, post, values, cot = [store[j].astype(f32) for store in stores]
        a_sum, b_sum = a_in[j][...].astype(f32), b_in[j][...].astype(f32)
        convolved, carried = jnp.where(half == 0, a_sum, b_sum), jnp.where(half == 0, b_sum, a_sum)
        for result, value in zip(results, (post * convolved, carried * values, cot * convolved, carried * pre)):
            result[j] = value.astype(bf16)
        for copy in copies(j, True):
            copy.start()
    for j in range(quarters):
        for copy in copies(j, True):
            copy.wait()


def swapped(pre_gate, post_gate, values, cotangent, filters):
    parts, dp_count = lax.axis_size("seq"), lax.axis_size("dp")
    quarters = parts // 2
    channels, groups = pre_gate.shape[2], filters.shape[1]
    width, local = channels // quarters, groups // quarters
    seq_index = lax.axis_index("seq")
    place = jnp.stack([seq_index // quarters, seq_index % quarters, lax.axis_index("dp")]).astype(jnp.int32)
    owners = parts * dp_count
    rows = filters.shape[0]
    f32, bf16 = jnp.float32, jnp.bfloat16
    every = ("dp", "seq")

    taps = filters.T
    pieces = [taps]
    for p in range(1, dp_count):
        pieces.append(lax.ppermute(taps, "dp", [(i, (i + p) % dp_count) for i in range(dp_count)]))

    gates = [pre_gate, post_gate, values, cotangent]
    lower = seq_index < quarters
    mixed = (pre_gate[0].astype(f32) * values[0]).astype(bf16)
    gated = (cotangent[0].astype(f32) * post_gate[0]).astype(bf16)
    a, b = jnp.where(lower, mixed, gated), jnp.where(lower, gated, mixed)
    store = pltpu.VMEM((quarters, BLOCK, width), bf16)
    message = jax.ShapeDtypeStruct((2 * BLOCK + TAIL, width), bf16)
    chunks = call(
        lambda *refs: pack_kernel(quarters, dp_count, *refs), "pack", place, pieces + [a, b],
        chunk_shapes(quarters, width) + [message] * quarters, [pltpu.VMEM((quarters, local, BLOCK), f32)],
        flops=1000, nbytes=1000,
    )
    a_own, ab_own = chunks[:quarters], chunks[quarters:]
    r_in = [swap(a_own[j], quarters + j) for j in range(quarters)]
    ab_in = [ab_own[0]] + [swap(ab_own[j], j) for j in range(1, quarters)]

    taps = jnp.concatenate([message[2 * BLOCK :, :BLOCK] for message in ab_in], axis=1)
    taps = [taps, swap(taps, quarters)]
    whole = (quarters, BLOCK, width)
    band = jax.ShapeDtypeStruct((local, 2 * BLOCK, K), bf16)
    *a_done, causal, anti, sums, lines = call(
        lambda *refs: local_kernel(quarters, dp_count, *refs), "local", place, taps + ab_in,
        chunk_shapes(quarters, width)
        + [band, band, jax.ShapeDtypeStruct(whole, f32), jax.ShapeDtypeStruct((local, K), f32)],
        [store] * 3 + [pltpu.VMEM((owners, local, rows), f32)], flops=1000, nbytes=1000,
        after=r_in[2:3],
    )
    a_back = [a_done[0]] + [swap(a_done[j], j) for j in range(1, quarters)]

    half_store = pltpu.VMEM((quarters, BLOCK, width // 2), bf16)
    shares, *b_done = call(
        lambda *refs: cross_kernel(quarters, *refs), "cross", place, ab_in + r_in + [lines, sums, causal, anti],
        [jax.ShapeDtypeStruct((owners, local, BLOCK), f32)] + chunk_shapes(quarters, width),
        [store] * 2 + [half_store] * 2 + [pltpu.VMEM((local, K), f32)], flops=1000, nbytes=1000,
        after=a_back[1:],
    )
    arrived = lax.all_to_all(shares, every, 0, 0, tiled=True)
    b_back = [b_done[0]] + [swap(b_done[j], j) for j in range(1, quarters)]

    shape = jax.ShapeDtypeStruct(pre_gate.shape, bf16)
    hbm = [pl.BlockSpec(memory_space=pltpu.HBM)] * 4
    output, grad_pre, grad_post, grad_values = pl.pallas_call(
        lambda *refs: outputs_kernel(quarters, *refs),
        in_specs=[pl.BlockSpec(memory_space=pltpu.SMEM)] + vmem_specs(2 * quarters) + hbm,
        out_specs=hbm,
        out_shape=[shape] * 4,
        scratch_shapes=[store] * 8 + [pltpu.SemaphoreType.DMA((quarters, 4))] * 2,
        compiler_params=pltpu.CompilerParams(vmem_limit_bytes=20 * 1024 * 1024),
        cost_estimate=pl.CostEstimate(flops=1000, bytes_accessed=1000, transcendentals=0),
        name="outputs",
    )(place, *a_back, *b_back, *gates)
    total = jnp.sum(arrived.reshape(owners // quarters, groups, BLOCK), axis=0)
    mine = lax.dynamic_slice_in_dim(total, (lax.axis_index(every) * rows) % BLOCK, rows, 1)
    total_tokens = dp_count * parts * pre_gate.shape[1] * (channels // groups)
    return output, grad_pre, grad_post, grad_values, mine.T / float(total_tokens**0.5)


def solution(mesh):
    def chosen(*shard):
        fits = swap_fits(*shard)
        return (swapped if fits else shards)(*shard)

    return jax.shard_map(
        chosen,
        mesh=mesh,
        in_specs=(
            P("dp", "seq", None),
            P("dp", "seq", None),
            P("dp", "seq", None),
            P("dp", "seq", None),
            P(("dp", "seq"), None),
        ),
        out_specs=(
            P("dp", "seq", None),
            P("dp", "seq", None),
            P("dp", "seq", None),
            P("dp", "seq", None),
            P(("dp", "seq"), None),
        ),
        check_vma=False,
    )
```

```python
import jax
import jax.numpy as jnp
import numpy as np
from jax import lax
from jax.experimental import pallas as pl
from jax.experimental.pallas import tpu as pltpu
from jax.sharding import PartitionSpec as P

K = 1024


def shifted(value, axis, steps):
    count = lax.axis_size(axis)
    first, last = (max(0, -steps), min(count, count - steps))
    return lax.ppermute(value, axis, [(source, source + steps) for source in range(first, last)])


def tile_index(lag_blocks, shard_len):
    offsets = np.arange(lag_blocks)[:, None, None] * shard_len
    rows_idx = np.arange(shard_len)[None, :, None]
    cols_idx = np.arange(shard_len)[None, None, :]
    return (offsets + rows_idx - cols_idx + shard_len).astype(np.int32)


def build_tiles(all_taps, lag_blocks, shard_len):
    tap_count = all_taps.shape[0]
    needed = (lag_blocks + 1) * shard_len
    trailing = max(needed - shard_len - tap_count, 0)
    padded = jnp.concatenate(
        [
            jnp.zeros((shard_len, all_taps.shape[1]), all_taps.dtype),
            all_taps,
            jnp.zeros((trailing, all_taps.shape[1]), all_taps.dtype),
        ],
        axis=0,
    )
    columns = padded.T
    return columns[:, tile_index(lag_blocks, shard_len)]


def earlier_relay(piece_in, history_len):

    def earlier_advance(moving, unused):
        arrived = shifted(moving, "seq", 1)
        return (arrived, arrived)

    unused_last, stacked = lax.scan(earlier_advance, piece_in, None, length=history_len)
    return jnp.concatenate([piece_in[None], stacked], axis=0)


def later_relay(piece_in, history_len):

    def later_advance(moving, unused):
        arrived = shifted(moving, "seq", -1)
        return (arrived, arrived)

    unused_last, stacked = lax.scan(later_advance, piece_in, None, length=history_len)
    return jnp.concatenate([piece_in[None], stacked], axis=0)


def lag_window(gated_rows, history, local_groups, group_width, lag_count):
    row_count = gated_rows.shape[0]
    span_len = history.shape[0]
    front_zero = jnp.zeros((row_count, history.shape[1]), history.dtype)
    widened = jnp.concatenate([front_zero, history], axis=0)
    gated_grp = gated_rows.reshape(row_count, local_groups, group_width).transpose(1, 0, 2)
    hist_grp = widened.reshape(span_len + row_count, local_groups, group_width).transpose(1, 0, 2)

    def one_group(pair_in):
        gated_one, hist_one = pair_in
        product = lax.dot_general(
            gated_one, hist_one, (((1,), (1,)), ((), ())), preferred_element_type=jnp.float32
        )
        padded = jnp.pad(product, ((0, 0), (0, row_count)))
        flat_line = jnp.concatenate(
            [padded.reshape(-1), jnp.zeros((row_count,), jnp.float32)], axis=0
        )
        skewed = flat_line.reshape(row_count, span_len + 2 * row_count + 1)
        diag_sums = jnp.sum(skewed, axis=0)
        return jnp.flip(diag_sums[1 : span_len + 1], axis=0)[:lag_count]

    return lax.map(one_group, (gated_grp, hist_grp))


def shards(pre_gate, post_gate, values, cotangent, filters):
    shard_len = pre_gate.shape[1]
    channels = pre_gate.shape[2]
    groups = filters.shape[1]
    group_size = channels // groups
    seq_count = lax.axis_size("seq")
    all_taps = lax.all_gather(filters, ("dp", "seq"), axis=0, tiled=True)
    mixed_in = (pre_gate[0].astype(jnp.float32) * values[0]).astype(jnp.bfloat16)
    gated = (cotangent[0].astype(jnp.float32) * post_gate[0]).astype(jnp.bfloat16)
    history_len = min(-(-K // shard_len), seq_count - 1)
    lag_blocks = history_len + 1
    mixed_ext = earlier_relay(mixed_in, history_len)
    gated_ext = later_relay(gated, history_len)
    mixed_four = mixed_ext.reshape(lag_blocks, shard_len, groups, group_size)
    gated_four = gated_ext.reshape(lag_blocks, shard_len, groups, group_size)
    tiles = build_tiles(all_taps, lag_blocks, shard_len)
    convolved = jnp.einsum(
        "gmij,mjgc->igc", tiles, mixed_four, preferred_element_type=jnp.float32
    ).reshape(shard_len, channels)
    carried = jnp.einsum(
        "gmji,mjgc->igc", tiles, gated_four, preferred_element_type=jnp.float32
    ).reshape(shard_len, channels)
    hist_len = lag_blocks * shard_len
    lag_count = min(K, hist_len)
    history = jnp.flip(mixed_ext, axis=0).reshape(hist_len, channels)
    lag_local = lag_window(gated, history, groups, group_size, lag_count)
    partial_grads = lag_local.T
    output = (post_gate[0].astype(jnp.float32) * convolved).astype(jnp.bfloat16)
    grad_post = (cotangent[0].astype(jnp.float32) * convolved).astype(jnp.bfloat16)
    grad_pre = (carried * values[0]).astype(jnp.bfloat16)
    grad_values = (carried * pre_gate[0]).astype(jnp.bfloat16)
    owned = lax.psum_scatter(partial_grads, ("dp", "seq"), scatter_dimension=0, tiled=True)
    total_tokens = lax.axis_size("dp") * shard_len * seq_count * group_size
    grad_filters = owned / float(total_tokens**0.5)
    return (output[None], grad_pre[None], grad_post[None], grad_values[None], grad_filters)


BLOCK = 128


def swap_fits(pre_gate, post_gate, values, cotangent, filters):
    parts, dp_count = lax.axis_size("seq"), lax.axis_size("dp")
    channels, groups = pre_gate.shape[2], filters.shape[1]
    return (
        parts >= 4
        and parts & (parts - 1) == 0
        and groups % parts == 0
        and channels // groups == BLOCK
        and pre_gate.shape[0] == 1
        and pre_gate.shape[1] == BLOCK
        and parts * BLOCK == K
        and filters.shape[0] * parts * dp_count == K
    )


def swap(chunk, flip):
    count = lax.axis_size("seq")
    return lax.ppermute(chunk, "seq", [(i, i ^ flip) for i in range(count)])


def vmem_specs(count):
    return [pl.BlockSpec(memory_space=pltpu.VMEM)] * count


def chunk_shapes(count, width, blocks=1):
    return [jax.ShapeDtypeStruct((blocks * BLOCK, width), jnp.bfloat16)] * count


def call(kernel, name, place, operands, out_shape, scratch=(), flops=1000, nbytes=1000, after=()):
    def body(place_ref, *refs):
        kernel(place_ref, *refs[: len(operands)], *refs[len(operands) + len(after) :])

    return pl.pallas_call(
        body,
        in_specs=[pl.BlockSpec(memory_space=pltpu.SMEM)]
        + vmem_specs(len(operands))
        + [pl.BlockSpec(memory_space=pl.ANY)] * len(after),
        out_specs=vmem_specs(len(out_shape)),
        out_shape=out_shape,
        scratch_shapes=list(scratch),
        compiler_params=pltpu.CompilerParams(vmem_limit_bytes=20 * 1024 * 1024),
        cost_estimate=pl.CostEstimate(flops=flops, bytes_accessed=nbytes, transcendentals=0),
        name=name,
    )(place, *operands, *after)


TAIL = 16


def pack_kernel(quarters, pieces, place_ref, *refs):
    f32, bf16 = jnp.float32, jnp.bfloat16
    taps_in, (a_ref, b_ref), refs = refs[:pieces], refs[pieces : pieces + 2], refs[pieces + 2 :]
    a_outs, outs, (taps_ref,) = refs[:quarters], refs[quarters : 2 * quarters], refs[2 * quarters :]
    quarter = place_ref[1]
    width = a_outs[0].shape[1]
    local = taps_ref.shape[1]
    taps = jnp.concatenate([piece[...].astype(f32) for piece in taps_in], axis=1)
    for i in range(quarters):
        taps_ref[i] = taps[i * local : (i + 1) * local]
    for j in range(quarters):
        columns = pl.ds(pl.multiple_of((quarter ^ j) * width, width), width)
        a = a_ref[:, columns]
        taps = taps_ref[quarter ^ j]
        taps = jnp.concatenate([taps, jnp.zeros((TAIL - local, BLOCK), f32)], axis=0)
        tail = jnp.concatenate([taps, jnp.zeros((TAIL, width - BLOCK), f32)], axis=1).astype(bf16)
        a_outs[j][:BLOCK] = a
        a_outs[j][BLOCK:] = tail
        outs[j][:BLOCK] = a
        outs[j][BLOCK : 2 * BLOCK] = b_ref[:, columns]
        outs[j][2 * BLOCK :] = tail


def bands(quarters, dp_count, place_ref, taps_in, taps_ref, causal_ref, anti_ref):
    half, quarter, dp_index = place_ref[0], place_ref[1], place_ref[2]
    local, rows = taps_ref.shape[1:]
    for u in range(2):
        for j in range(quarters):
            piece = taps_in[u * quarters + j][-TAIL:, :BLOCK].astype(jnp.float32)
            for p in range(dp_count):
                owner = lax.rem(dp_index + dp_count - p, dp_count) * 2 * quarters + (half ^ u) * quarters + (quarter ^ j)
                start = p * rows
                taps_ref[owner] = piece[:local, start : start + rows]
    for g in range(local):
        line = jnp.concatenate([taps_ref[o, g : g + 1] for o in range(taps_ref.shape[0])], axis=1)
        line = jnp.concatenate([line, jnp.zeros((1, BLOCK), jnp.float32)], axis=1)
        shear = pltpu.roll(jnp.broadcast_to(line, (BLOCK, K + BLOCK)), 0, 1, stride=1, stride_axis=0)
        zero = jnp.zeros((BLOCK, BLOCK), jnp.bfloat16)
        count = K // BLOCK
        tiles = [shear[:, m * BLOCK : (m + 1) * BLOCK] for m in range(count)]
        for b in range(count):
            columns = slice(b * BLOCK, (b + 1) * BLOCK)
            anti_ref[g, :BLOCK, columns] = tiles[b].astype(jnp.bfloat16)
            anti_ref[g, BLOCK:, columns] = tiles[b - 1].astype(jnp.bfloat16) if b else zero
        turned = [tile.T.astype(jnp.bfloat16) for tile in tiles] + [zero]
        for b in range(count):
            columns = slice(b * BLOCK, (b + 1) * BLOCK)
            causal_ref[g, :BLOCK, columns] = turned[count - 2 - b]
            causal_ref[g, BLOCK:, columns] = turned[count - 1 - b]


def rows_of(ref, lanes):
    return ref[:, :, lanes].reshape(ref.shape[0] * BLOCK, BLOCK)


def dot(left, right):
    return jnp.dot(left, right, preferred_element_type=jnp.float32)


def causal_part(band, data, p):
    reach = (p + 1) * 2 * BLOCK
    return dot(band[:, K - reach :], data[:reach])


def anti_part(band, data, p):
    return dot(band[:, : data.shape[0] - p * 2 * BLOCK], data[p * 2 * BLOCK :])


def lag_lines(mixed, mixed_first, gated, gated_first, turn):
    count = mixed.shape[0] // BLOCK
    blocks = K // BLOCK
    turned = jnp.concatenate(
        [dot(turn, mixed[j * BLOCK : (j + 1) * BLOCK]).astype(jnp.bfloat16) for j in range(count)], axis=0
    )
    sums = [None] * blocks
    for i in range(gated.shape[0] // BLOCK):
        first = gated_first + i - mixed_first
        top = min(count, first + 1)
        product = lax.dot_general(
            turned[: top * BLOCK],
            gated[i * BLOCK : (i + 1) * BLOCK],
            (((1,), (1,)), ((), ())),
            preferred_element_type=jnp.float32,
        )
        for j in range(top):
            term = product[j * BLOCK : (j + 1) * BLOCK]
            sums[first - j] = term if sums[first - j] is None else sums[first - j] + term
    last = max(m for m in range(blocks) if sums[m] is not None)
    table = jnp.concatenate(sums[: last + 1] + [jnp.zeros((BLOCK, BLOCK), jnp.float32)], axis=1)
    span = (last + 2) * BLOCK
    shear = jnp.sum(pltpu.roll(table, 0, 1, stride=1, stride_axis=0), axis=0, keepdims=True)
    if span < K:
        shear = jnp.concatenate([shear, jnp.zeros((1, K + BLOCK - span), jnp.float32)], axis=1)
    return pltpu.roll(shear, K + BLOCK - (BLOCK - 1), 1)[:, :K]


def exchange():
    rows = lax.broadcasted_iota(jnp.int32, (BLOCK, BLOCK), 0)
    columns = lax.broadcasted_iota(jnp.int32, (BLOCK, BLOCK), 1)
    return jnp.where(rows + columns == BLOCK - 1, 1.0, 0.0).astype(jnp.bfloat16)


def gather(quarters, place_ref, ab_in, r_in, a_ref, data_ref):
    half, quarter = place_ref[0], place_ref[1]
    for j in range(quarters):
        a_ref[quarter ^ j] = ab_in[j][:BLOCK]
        data_ref[half * quarters + (quarter ^ j)] = ab_in[j][BLOCK : 2 * BLOCK]
        data_ref[(1 - half) * quarters + (quarter ^ j)] = r_in[j][:BLOCK]


def lags_kernel(quarters, place_ref, *refs):
    ab_in, r_in, refs = refs[:quarters], refs[quarters : 2 * quarters], refs[2 * quarters :]
    shares_ref, a_ref, data_ref, lines_ref = refs
    gather(quarters, place_ref, ab_in, r_in, a_ref, data_ref)
    half = place_ref[0]
    turn = exchange()
    local = lines_ref.shape[0]
    length = quarters * BLOCK

    @pl.when(half == 0)
    def lower():
        for g in range(local):
            lanes = slice(g * BLOCK, (g + 1) * BLOCK)
            mixed, gated = rows_of(a_ref, lanes), rows_of(data_ref, lanes)
            lines_ref[g : g + 1] = lag_lines(mixed, 0, gated if g < local // 2 else gated[:length], 0, turn)

    @pl.when(half != 0)
    def upper():
        for g in range(local):
            lanes = slice(g * BLOCK, (g + 1) * BLOCK)
            gated, mixed = rows_of(a_ref, lanes), rows_of(data_ref, lanes)
            first = quarters if g < local // 2 else 0
            lines_ref[g : g + 1] = lag_lines(mixed[first * BLOCK :], first, gated, quarters, turn)

    step = BLOCK // local
    lane = lax.broadcasted_iota(jnp.int32, (1, K), 1) % BLOCK // step
    for u in range(local):
        row = jnp.zeros((1, K), jnp.float32)
        for g in range(local):
            row = jnp.where(lane == g, pltpu.roll(lines_ref[g : g + 1], (g - u) * step % K, 1), row)
        for block in range(K // BLOCK):
            shares_ref[block * local + u : block * local + u + 1] = row[:, block * BLOCK : (block + 1) * BLOCK]


def sums_kernel(quarters, dp_count, place_ref, *refs):
    ab_in, r_in, outs, refs = refs[:quarters], refs[quarters : 2 * quarters], refs[2 * quarters : 3 * quarters], refs[3 * quarters :]
    causal_ref, anti_ref, a_ref, data_ref, a_sum_ref, b_sum_ref, taps_ref = refs
    gather(quarters, place_ref, ab_in, r_in, a_ref, data_ref)
    bands(quarters, dp_count, place_ref, ab_in + r_in, taps_ref, causal_ref, anti_ref)
    half, quarter = place_ref[0], place_ref[1]

    def work(a_part, a_band, b_part, b_band, first):
        for g in range(causal_ref.shape[0]):
            lanes = slice(g * BLOCK, (g + 1) * BLOCK)
            a_rows, data = rows_of(a_ref, lanes), rows_of(data_ref, lanes)
            for p in range(quarters // 2):
                pair = slice(2 * p, 2 * p + 2)
                a_sum = a_part(a_band.at[g], a_rows, p)
                a_sum_ref[pair, :, lanes] = a_sum.reshape(2, BLOCK, BLOCK).astype(jnp.bfloat16)
                b_sum = b_part(b_band.at[g], data, first + p)
                b_sum_ref[pair, :, lanes] = b_sum.reshape(2, BLOCK, BLOCK).astype(jnp.bfloat16)

    @pl.when(half == 0)
    def lower():
        work(causal_part, causal_ref, anti_part, anti_ref, 0)

    @pl.when(half != 0)
    def upper():
        work(anti_part, anti_ref, causal_part, causal_ref, quarters // 2)

    for j in range(quarters):
        outs[j][:BLOCK] = a_sum_ref[quarter ^ j]
        outs[j][BLOCK:] = b_sum_ref[quarter ^ j]


def owned_kernel(scale, place_ref, arrived_ref, out_ref):
    groups, rows = out_ref.shape
    local = BLOCK // rows
    quarters = groups // local
    total = arrived_ref[:quarters]
    for i in range(1, arrived_ref.shape[0] // quarters):
        total = total + arrived_ref[i * quarters : (i + 1) * quarters]
    total = total * scale
    for g in range(local):
        part = (total if g == 0 else pltpu.roll(total, BLOCK - g * rows, 1))[:, :rows]
        for q in range(quarters):
            out_ref[q * local + g : q * local + g + 1] = part[q : q + 1]


def outputs_kernel(quarters, place_ref, *refs):
    f32, bf16 = jnp.float32, jnp.bfloat16
    back, inputs, refs = refs[:quarters], refs[quarters : quarters + 4], refs[quarters + 4 :]
    outputs, results, sem = refs[:4], refs[4:8], refs[8]
    half, quarter = place_ref[0], place_ref[1]
    width = back[0].shape[1]

    def copies(j, columns):
        return [
            pltpu.make_async_copy(store.at[j], target.at[0, :, columns], sem.at[j, i])
            for i, (store, target) in enumerate(zip(results, outputs))
        ]

    def place(j):
        return pl.ds(pl.multiple_of((quarter ^ j) * width, width), width)

    for j in range(quarters):
        columns = place(j)
        pre, post, values, cot = [source[0, :, columns].astype(f32) for source in inputs]
        a_sum, b_sum = back[j][:BLOCK].astype(f32), back[j][BLOCK:].astype(f32)
        convolved, carried = jnp.where(half == 0, a_sum, b_sum), jnp.where(half == 0, b_sum, a_sum)
        for result, value in zip(results, (post * convolved, carried * values, cot * convolved, carried * pre)):
            result[j] = value.astype(bf16)
        for copy in copies(j, columns):
            copy.start()
    for j in range(quarters):
        for copy in copies(j, place(j)):
            copy.wait()


def swapped(pre_gate, post_gate, values, cotangent, filters):
    parts, dp_count = lax.axis_size("seq"), lax.axis_size("dp")
    quarters = parts // 2
    channels, groups = pre_gate.shape[2], filters.shape[1]
    width, local = channels // quarters, groups // quarters
    seq_index = lax.axis_index("seq")
    place = jnp.stack([seq_index // quarters, seq_index % quarters, lax.axis_index("dp")]).astype(jnp.int32)
    owners = parts * dp_count
    rows = filters.shape[0]
    f32, bf16 = jnp.float32, jnp.bfloat16
    every = ("dp", "seq")

    taps = filters.T
    pieces = [taps]
    for p in range(1, dp_count):
        pieces.append(lax.ppermute(taps, "dp", [(i, (i + p) % dp_count) for i in range(dp_count)]))

    gates = [pre_gate, post_gate, values, cotangent]
    lower = seq_index < quarters
    mixed = (pre_gate[0].astype(f32) * values[0]).astype(bf16)
    gated = (cotangent[0].astype(f32) * post_gate[0]).astype(bf16)
    a, b = jnp.where(lower, mixed, gated), jnp.where(lower, gated, mixed)
    store = pltpu.VMEM((quarters, BLOCK, width), bf16)
    short = jax.ShapeDtypeStruct((BLOCK + TAIL, width), bf16)
    message = jax.ShapeDtypeStruct((2 * BLOCK + TAIL, width), bf16)
    chunks = call(
        lambda *refs: pack_kernel(quarters, dp_count, *refs), "pack", place, pieces + [a, b],
        [short] * quarters + [message] * quarters, [pltpu.VMEM((quarters, local, BLOCK), f32)],
        flops=1000, nbytes=1000,
    )
    a_own, ab_own = chunks[:quarters], chunks[quarters:]
    r_in = [swap(a_own[j], quarters + j) for j in range(quarters)]
    ab_in = [ab_own[0]] + [swap(ab_own[j], j) for j in range(1, quarters)]

    band = pltpu.VMEM((local, 2 * BLOCK, K), bf16)
    store = pltpu.VMEM((quarters, BLOCK, width), bf16)
    whole = pltpu.VMEM((parts, BLOCK, width), bf16)
    done = call(
        lambda *refs: sums_kernel(quarters, dp_count, *refs), "sums", place, ab_in + r_in, chunk_shapes(quarters, width, 2),
        [band, band, store, whole, store, store, pltpu.VMEM((owners, local, rows), f32)], flops=1000, nbytes=1000,
    )
    back = [done[0]] + [swap(done[j], j) for j in range(1, quarters)]
    token = lax.ppermute(done[0], "dp", [(i, i ^ 1) for i in range(dp_count)])
    (shares,) = call(
        lambda *refs: lags_kernel(quarters, *refs), "lags", place, ab_in + r_in,
        [jax.ShapeDtypeStruct((owners, BLOCK), f32)], [store, whole, pltpu.VMEM((local, K), f32)],
        flops=1000, nbytes=1000, after=[token],
    )
    arrived = lax.all_to_all(shares, every, 0, 0, tiled=True)

    shape = jax.ShapeDtypeStruct(pre_gate.shape, bf16)
    hbm = [pl.BlockSpec(memory_space=pltpu.HBM)] * 4
    output, grad_pre, grad_post, grad_values = pl.pallas_call(
        lambda *refs: outputs_kernel(quarters, *refs),
        in_specs=[pl.BlockSpec(memory_space=pltpu.SMEM)] + vmem_specs(quarters + 4),
        out_specs=hbm,
        out_shape=[shape] * 4,
        scratch_shapes=[store] * 4 + [pltpu.SemaphoreType.DMA((quarters, 4))],
        compiler_params=pltpu.CompilerParams(vmem_limit_bytes=20 * 1024 * 1024),
        cost_estimate=pl.CostEstimate(flops=1000, bytes_accessed=1000, transcendentals=0),
        name="outputs",
    )(place, *back, *gates)
    total_tokens = dp_count * parts * pre_gate.shape[1] * (channels // groups)
    (mine,) = call(
        lambda *refs: owned_kernel(1.0 / float(total_tokens**0.5), *refs), "owned", place, [arrived],
        [jax.ShapeDtypeStruct((groups, rows), f32)], flops=1000, nbytes=1000,
    )
    return output, grad_pre, grad_post, grad_values, mine.T


def solution(mesh):
    def chosen(*shard):
        fits = swap_fits(*shard)
        return (swapped if fits else shards)(*shard)

    return jax.shard_map(
        chosen,
        mesh=mesh,
        in_specs=(
            P("dp", "seq", None),
            P("dp", "seq", None),
            P("dp", "seq", None),
            P("dp", "seq", None),
            P(("dp", "seq"), None),
        ),
        out_specs=(
            P("dp", "seq", None),
            P("dp", "seq", None),
            P("dp", "seq", None),
            P("dp", "seq", None),
            P(("dp", "seq"), None),
        ),
        check_vma=False,
    )
```

```python
import jax
import jax.numpy as jnp
import numpy as np
from jax import lax
from jax.experimental import pallas as pl
from jax.experimental.pallas import tpu as pltpu
from jax.sharding import PartitionSpec as P

K = 1024


def shifted(value, axis, steps):
    count = lax.axis_size(axis)
    first, last = (max(0, -steps), min(count, count - steps))
    return lax.ppermute(value, axis, [(source, source + steps) for source in range(first, last)])


def tile_index(lag_blocks, shard_len):
    offsets = np.arange(lag_blocks)[:, None, None] * shard_len
    rows_idx = np.arange(shard_len)[None, :, None]
    cols_idx = np.arange(shard_len)[None, None, :]
    return (offsets + rows_idx - cols_idx + shard_len).astype(np.int32)


def build_tiles(all_taps, lag_blocks, shard_len):
    tap_count = all_taps.shape[0]
    needed = (lag_blocks + 1) * shard_len
    trailing = max(needed - shard_len - tap_count, 0)
    padded = jnp.concatenate(
        [
            jnp.zeros((shard_len, all_taps.shape[1]), all_taps.dtype),
            all_taps,
            jnp.zeros((trailing, all_taps.shape[1]), all_taps.dtype),
        ],
        axis=0,
    )
    columns = padded.T
    return columns[:, tile_index(lag_blocks, shard_len)]


def earlier_relay(piece_in, history_len):

    def earlier_advance(moving, unused):
        arrived = shifted(moving, "seq", 1)
        return (arrived, arrived)

    unused_last, stacked = lax.scan(earlier_advance, piece_in, None, length=history_len)
    return jnp.concatenate([piece_in[None], stacked], axis=0)


def later_relay(piece_in, history_len):

    def later_advance(moving, unused):
        arrived = shifted(moving, "seq", -1)
        return (arrived, arrived)

    unused_last, stacked = lax.scan(later_advance, piece_in, None, length=history_len)
    return jnp.concatenate([piece_in[None], stacked], axis=0)


def lag_window(gated_rows, history, local_groups, group_width, lag_count):
    row_count = gated_rows.shape[0]
    span_len = history.shape[0]
    front_zero = jnp.zeros((row_count, history.shape[1]), history.dtype)
    widened = jnp.concatenate([front_zero, history], axis=0)
    gated_grp = gated_rows.reshape(row_count, local_groups, group_width).transpose(1, 0, 2)
    hist_grp = widened.reshape(span_len + row_count, local_groups, group_width).transpose(1, 0, 2)

    def one_group(pair_in):
        gated_one, hist_one = pair_in
        product = lax.dot_general(
            gated_one, hist_one, (((1,), (1,)), ((), ())), preferred_element_type=jnp.float32
        )
        padded = jnp.pad(product, ((0, 0), (0, row_count)))
        flat_line = jnp.concatenate(
            [padded.reshape(-1), jnp.zeros((row_count,), jnp.float32)], axis=0
        )
        skewed = flat_line.reshape(row_count, span_len + 2 * row_count + 1)
        diag_sums = jnp.sum(skewed, axis=0)
        return jnp.flip(diag_sums[1 : span_len + 1], axis=0)[:lag_count]

    return lax.map(one_group, (gated_grp, hist_grp))


def shards(pre_gate, post_gate, values, cotangent, filters):
    shard_len = pre_gate.shape[1]
    channels = pre_gate.shape[2]
    groups = filters.shape[1]
    group_size = channels // groups
    seq_count = lax.axis_size("seq")
    all_taps = lax.all_gather(filters, ("dp", "seq"), axis=0, tiled=True)
    mixed_in = (pre_gate[0].astype(jnp.float32) * values[0]).astype(jnp.bfloat16)
    gated = (cotangent[0].astype(jnp.float32) * post_gate[0]).astype(jnp.bfloat16)
    history_len = min(-(-K // shard_len), seq_count - 1)
    lag_blocks = history_len + 1
    mixed_ext = earlier_relay(mixed_in, history_len)
    gated_ext = later_relay(gated, history_len)
    mixed_four = mixed_ext.reshape(lag_blocks, shard_len, groups, group_size)
    gated_four = gated_ext.reshape(lag_blocks, shard_len, groups, group_size)
    tiles = build_tiles(all_taps, lag_blocks, shard_len)
    convolved = jnp.einsum(
        "gmij,mjgc->igc", tiles, mixed_four, preferred_element_type=jnp.float32
    ).reshape(shard_len, channels)
    carried = jnp.einsum(
        "gmji,mjgc->igc", tiles, gated_four, preferred_element_type=jnp.float32
    ).reshape(shard_len, channels)
    hist_len = lag_blocks * shard_len
    lag_count = min(K, hist_len)
    history = jnp.flip(mixed_ext, axis=0).reshape(hist_len, channels)
    lag_local = lag_window(gated, history, groups, group_size, lag_count)
    partial_grads = lag_local.T
    output = (post_gate[0].astype(jnp.float32) * convolved).astype(jnp.bfloat16)
    grad_post = (cotangent[0].astype(jnp.float32) * convolved).astype(jnp.bfloat16)
    grad_pre = (carried * values[0]).astype(jnp.bfloat16)
    grad_values = (carried * pre_gate[0]).astype(jnp.bfloat16)
    owned = lax.psum_scatter(partial_grads, ("dp", "seq"), scatter_dimension=0, tiled=True)
    total_tokens = lax.axis_size("dp") * shard_len * seq_count * group_size
    grad_filters = owned / float(total_tokens**0.5)
    return (output[None], grad_pre[None], grad_post[None], grad_values[None], grad_filters)


BLOCK = 128


def swap_fits(pre_gate, post_gate, values, cotangent, filters):
    parts, dp_count = lax.axis_size("seq"), lax.axis_size("dp")
    channels, groups = pre_gate.shape[2], filters.shape[1]
    return (
        parts >= 4
        and parts & (parts - 1) == 0
        and groups % parts == 0
        and channels // groups == BLOCK
        and pre_gate.shape[0] == 1
        and pre_gate.shape[1] == BLOCK
        and parts * BLOCK == K
        and filters.shape[0] * parts * dp_count == K
    )


def swap(chunk, flip):
    count = lax.axis_size("seq")
    return lax.ppermute(chunk, "seq", [(i, i ^ flip) for i in range(count)])


def vmem_specs(count):
    return [pl.BlockSpec(memory_space=pltpu.VMEM)] * count


def chunk_shapes(count, width, blocks=1):
    return [jax.ShapeDtypeStruct((blocks * BLOCK, width), jnp.bfloat16)] * count


def call(kernel, name, place, operands, out_shape, scratch=(), flops=1000, nbytes=1000, after=()):
    def body(place_ref, *refs):
        kernel(place_ref, *refs[: len(operands)], *refs[len(operands) + len(after) :])

    return pl.pallas_call(
        body,
        in_specs=[pl.BlockSpec(memory_space=pltpu.SMEM)]
        + vmem_specs(len(operands))
        + [pl.BlockSpec(memory_space=pl.ANY)] * len(after),
        out_specs=vmem_specs(len(out_shape)),
        out_shape=out_shape,
        scratch_shapes=list(scratch),
        compiler_params=pltpu.CompilerParams(vmem_limit_bytes=20 * 1024 * 1024),
        cost_estimate=pl.CostEstimate(flops=flops, bytes_accessed=nbytes, transcendentals=0),
        name=name,
    )(place, *operands, *after)


TAIL = 16


def pack_kernel(quarters, pieces, place_ref, *refs):
    f32, bf16 = jnp.float32, jnp.bfloat16
    taps_in, (a_ref, b_ref), refs = refs[:pieces], refs[pieces : pieces + 2], refs[pieces + 2 :]
    a_outs, outs, (taps_ref,) = refs[:quarters], refs[quarters : 2 * quarters], refs[2 * quarters :]
    quarter = place_ref[1]
    local = taps_ref.shape[1]
    taps = jnp.concatenate([piece[...].astype(f32) for piece in taps_in], axis=1)
    for i in range(quarters):
        taps_ref[i] = taps[i * local : (i + 1) * local]
    for j in range(quarters):
        for g in range(local):
            columns = pl.ds(pl.multiple_of(((quarter ^ j) * local + g) * BLOCK, BLOCK), BLOCK)
            a = a_ref[:, columns]
            a_outs[j][g * BLOCK : (g + 1) * BLOCK] = a
            if j < quarters - 1:
                outs[j][g * BLOCK : (g + 1) * BLOCK] = a
                outs[j][(local + g) * BLOCK : (local + g + 1) * BLOCK] = b_ref[:, columns]
            else:
                outs[j][g * BLOCK : (g + 1) * BLOCK] = b_ref[:, columns]
        tail = jnp.concatenate([taps_ref[quarter ^ j], jnp.zeros((TAIL - local, BLOCK), f32)], axis=0).astype(bf16)
        a_outs[j][local * BLOCK :] = tail
        outs[j][-TAIL:] = tail


def bands(quarters, dp_count, place_ref, taps_in, taps_ref, causal_ref, anti_ref, causal_from, anti_to):
    half, quarter, dp_index = place_ref[0], place_ref[1], place_ref[2]
    local, rows = taps_ref.shape[1:]
    for u in range(2):
        for j in range(quarters):
            piece = taps_in[u * quarters + j][-TAIL:].astype(jnp.float32)
            for p in range(dp_count):
                owner = lax.rem(dp_index + dp_count - p, dp_count) * 2 * quarters + (half ^ u) * quarters + (quarter ^ j)
                start = p * rows
                taps_ref[owner] = piece[:local, start : start + rows]
    for g in range(local):
        line = jnp.concatenate([taps_ref[o, g : g + 1] for o in range(taps_ref.shape[0])], axis=1)
        line = jnp.concatenate([line, jnp.zeros((1, BLOCK), jnp.float32)], axis=1)
        shear = pltpu.roll(jnp.broadcast_to(line, (BLOCK, K + BLOCK)), 0, 1, stride=1, stride_axis=0)
        zero = jnp.zeros((BLOCK, BLOCK), jnp.bfloat16)
        count = K // BLOCK
        tiles = [shear[:, m * BLOCK : (m + 1) * BLOCK] for m in range(count)]
        for b in range(anti_to // BLOCK):
            columns = slice(b * BLOCK, (b + 1) * BLOCK)
            anti_ref[g, :BLOCK, columns] = tiles[b].astype(jnp.bfloat16)
            anti_ref[g, BLOCK:, columns] = tiles[b - 1].astype(jnp.bfloat16) if b else zero
        wanted = count - causal_from // BLOCK
        turned = [tile.T.astype(jnp.bfloat16) for tile in tiles[:wanted]] + [zero]
        for b in range(count - wanted, count):
            columns = slice(b * BLOCK, (b + 1) * BLOCK)
            causal_ref[g, :BLOCK, columns] = turned[count - 2 - b] if b < count - 1 else zero
            causal_ref[g, BLOCK:, columns] = turned[count - 1 - b]


def rows_of(ref, lanes):
    return ref[:, :, lanes].reshape(ref.shape[0] * BLOCK, BLOCK)


def dot(left, right):
    return jnp.dot(left, right, preferred_element_type=jnp.float32)


def causal_part(band, data, p):
    reach = (p + 1) * 2 * BLOCK
    return dot(band[:, K - reach :], data[:reach])


def anti_part(band, data, p):
    return dot(band[:, : data.shape[0] - p * 2 * BLOCK], data[p * 2 * BLOCK :])


def lag_lines(mixed, mixed_first, gated, gated_first, turn):
    count = mixed.shape[0] // BLOCK
    blocks = K // BLOCK
    turned = jnp.concatenate(
        [dot(turn, mixed[j * BLOCK : (j + 1) * BLOCK]).astype(jnp.bfloat16) for j in range(count)], axis=0
    )
    sums = [None] * blocks
    for i in range(gated.shape[0] // BLOCK):
        first = gated_first + i - mixed_first
        top = min(count, first + 1)
        product = lax.dot_general(
            turned[: top * BLOCK],
            gated[i * BLOCK : (i + 1) * BLOCK],
            (((1,), (1,)), ((), ())),
            preferred_element_type=jnp.float32,
        )
        for j in range(top):
            term = product[j * BLOCK : (j + 1) * BLOCK]
            sums[first - j] = term if sums[first - j] is None else sums[first - j] + term
    last = max(m for m in range(blocks) if sums[m] is not None)
    table = jnp.concatenate(sums[: last + 1] + [jnp.zeros((BLOCK, BLOCK), jnp.float32)], axis=1)
    span = (last + 2) * BLOCK
    shear = jnp.sum(pltpu.roll(table, 0, 1, stride=1, stride_axis=0), axis=0, keepdims=True)
    if span < K:
        shear = jnp.concatenate([shear, jnp.zeros((1, K + BLOCK - span), jnp.float32)], axis=1)
    return pltpu.roll(shear, K + BLOCK - (BLOCK - 1), 1)[:, :K]


def exchange():
    rows = lax.broadcasted_iota(jnp.int32, (BLOCK, BLOCK), 0)
    columns = lax.broadcasted_iota(jnp.int32, (BLOCK, BLOCK), 1)
    return jnp.where(rows + columns == BLOCK - 1, 1.0, 0.0).astype(jnp.bfloat16)


def gather(quarters, place_ref, ab_in, r_in, a_ref, data_ref):
    half, quarter = place_ref[0], place_ref[1]
    local = a_ref.shape[2] // BLOCK
    for j in range(quarters):
        b_in, b_row = (ab_in[j], local) if j < quarters - 1 else (ab_in[j + 1], 0)
        for g in range(local):
            lanes = slice(g * BLOCK, (g + 1) * BLOCK)
            a_ref[quarter ^ j, :, lanes] = ab_in[j][g * BLOCK : (g + 1) * BLOCK]
            b_rows = slice((b_row + g) * BLOCK, (b_row + g + 1) * BLOCK)
            data_ref[half * quarters + (quarter ^ j), :, lanes] = b_in[b_rows]
            data_ref[(1 - half) * quarters + (quarter ^ j), :, lanes] = r_in[j][g * BLOCK : (g + 1) * BLOCK]


def lags_kernel(quarters, place_ref, *refs):
    ab_in, r_in, refs = refs[: quarters + 1], refs[quarters + 1 : 2 * quarters + 1], refs[2 * quarters + 1 :]
    shares_ref, a_ref, data_ref, lines_ref = refs
    gather(quarters, place_ref, ab_in, r_in, a_ref, data_ref)
    half = place_ref[0]
    turn = exchange()
    local = lines_ref.shape[0]
    length = quarters * BLOCK

    @pl.when(half == 0)
    def lower():
        for g in range(local):
            lanes = slice(g * BLOCK, (g + 1) * BLOCK)
            mixed, gated = rows_of(a_ref, lanes), rows_of(data_ref, lanes)
            lines_ref[g : g + 1] = lag_lines(mixed, 0, gated if g < local // 2 else gated[:length], 0, turn)

    @pl.when(half != 0)
    def upper():
        for g in range(local):
            lanes = slice(g * BLOCK, (g + 1) * BLOCK)
            gated, mixed = rows_of(a_ref, lanes), rows_of(data_ref, lanes)
            first = quarters if g < local // 2 else 0
            lines_ref[g : g + 1] = lag_lines(mixed[first * BLOCK :], first, gated, quarters, turn)

    step = BLOCK // local
    lane = lax.broadcasted_iota(jnp.int32, (1, K), 1) % BLOCK // step
    for u in range(local):
        row = jnp.zeros((1, K), jnp.float32)
        for g in range(local):
            row = jnp.where(lane == g, pltpu.roll(lines_ref[g : g + 1], (g - u) * step % K, 1), row)
        for block in range(K // BLOCK):
            shares_ref[block * local + u : block * local + u + 1] = row[:, block * BLOCK : (block + 1) * BLOCK]


def sums_kernel(quarters, dp_count, place_ref, *refs):
    ab_in, r_in, refs = refs[: quarters + 1], refs[quarters + 1 : 2 * quarters + 1], refs[2 * quarters + 1 :]
    outs, refs = refs[:quarters], refs[quarters:]
    causal_ref, anti_ref, a_ref, data_ref, a_sum_ref, b_sum_ref, taps_ref = refs
    gather(quarters, place_ref, ab_in, r_in, a_ref, data_ref)
    tails = ab_in[:quarters] + r_in
    half, quarter = place_ref[0], place_ref[1]

    def work(a_part, a_band, b_part, b_band, first):
        for g in range(causal_ref.shape[0]):
            lanes = slice(g * BLOCK, (g + 1) * BLOCK)
            a_rows, data = rows_of(a_ref, lanes), rows_of(data_ref, lanes)
            for p in range(quarters // 2):
                pair = slice(2 * p, 2 * p + 2)
                a_sum = a_part(a_band.at[g], a_rows, p)
                a_sum_ref[pair, :, lanes] = a_sum.reshape(2, BLOCK, BLOCK).astype(jnp.bfloat16)
                b_sum = b_part(b_band.at[g], data, first + p)
                b_sum_ref[pair, :, lanes] = b_sum.reshape(2, BLOCK, BLOCK).astype(jnp.bfloat16)

    @pl.when(half == 0)
    def lower():
        bands(quarters, dp_count, place_ref, tails, taps_ref, causal_ref, anti_ref, K // 2, K)
        work(causal_part, causal_ref, anti_part, anti_ref, 0)

    @pl.when(half != 0)
    def upper():
        bands(quarters, dp_count, place_ref, tails, taps_ref, causal_ref, anti_ref, 0, K // 2)
        work(anti_part, anti_ref, causal_part, causal_ref, quarters // 2)

    for j in range(quarters):
        outs[j][:BLOCK] = a_sum_ref[quarter ^ j]
        outs[j][BLOCK:] = b_sum_ref[quarter ^ j]


def owned_kernel(scale, place_ref, arrived_ref, out_ref):
    groups, rows = out_ref.shape
    local = BLOCK // rows
    quarters = groups // local
    total = arrived_ref[:quarters]
    for i in range(1, arrived_ref.shape[0] // quarters):
        total = total + arrived_ref[i * quarters : (i + 1) * quarters]
    total = total * scale
    for g in range(local):
        part = (total if g == 0 else pltpu.roll(total, BLOCK - g * rows, 1))[:, :rows]
        for q in range(quarters):
            out_ref[q * local + g : q * local + g + 1] = part[q : q + 1]


def outputs_kernel(js, place_ref, *refs):
    f32, bf16 = jnp.float32, jnp.bfloat16
    count = len(js)
    back, inputs = refs[:count], refs[count : count + 4]
    outputs, results, sem = refs[-9:-5], refs[-5:-1], refs[-1]
    half, quarter = place_ref[0], place_ref[1]
    width = back[0].shape[1]

    def place(j):
        return pl.ds(pl.multiple_of((quarter ^ j) * width, width), width)

    def copies(i):
        return [
            pltpu.make_async_copy(store.at[i], target.at[0, :, place(js[i])], sem.at[i, k])
            for k, (store, target) in enumerate(zip(results, outputs))
        ]

    for i in range(count):
        columns = place(js[i])
        pre, post, values, cot = [source[0, :, columns].astype(f32) for source in inputs]
        a_sum, b_sum = back[i][:BLOCK].astype(f32), back[i][BLOCK:].astype(f32)
        convolved, carried = jnp.where(half == 0, a_sum, b_sum), jnp.where(half == 0, b_sum, a_sum)
        for result, value in zip(results, (post * convolved, carried * values, cot * convolved, carried * pre)):
            result[i] = value.astype(bf16)
        for copy in copies(i):
            copy.start()
    for i in range(count):
        for copy in copies(i):
            copy.wait()


def gate_outputs(js, place, back, gates, earlier=()):
    hbm = [pl.BlockSpec(memory_space=pltpu.HBM)] * 4
    store = pltpu.VMEM((len(js), BLOCK, back[0].shape[1]), jnp.bfloat16)
    return pl.pallas_call(
        lambda *refs: outputs_kernel(js, *refs),
        in_specs=[pl.BlockSpec(memory_space=pltpu.SMEM)] + vmem_specs(len(js) + 4) + hbm[: len(earlier)],
        out_specs=hbm,
        out_shape=[jax.ShapeDtypeStruct(gates[0].shape, jnp.bfloat16)] * 4,
        input_output_aliases={1 + len(js) + 4 + k: k for k in range(len(earlier))},
        scratch_shapes=[store] * 4 + [pltpu.SemaphoreType.DMA((len(js), 4))],
        compiler_params=pltpu.CompilerParams(vmem_limit_bytes=20 * 1024 * 1024),
        cost_estimate=pl.CostEstimate(flops=1000, bytes_accessed=1000, transcendentals=0),
        name="outputs",
    )(place, *[back[j] for j in js], *gates, *earlier)


def swapped(pre_gate, post_gate, values, cotangent, filters):
    parts, dp_count = lax.axis_size("seq"), lax.axis_size("dp")
    quarters = parts // 2
    channels, groups = pre_gate.shape[2], filters.shape[1]
    width, local = channels // quarters, groups // quarters
    seq_index = lax.axis_index("seq")
    place = jnp.stack([seq_index // quarters, seq_index % quarters, lax.axis_index("dp")]).astype(jnp.int32)
    owners = parts * dp_count
    rows = filters.shape[0]
    f32, bf16 = jnp.float32, jnp.bfloat16
    every = ("dp", "seq")

    taps = filters.T
    pieces = [taps]
    for p in range(1, dp_count):
        pieces.append(lax.ppermute(taps, "dp", [(i, (i + p) % dp_count) for i in range(dp_count)]))

    gates = [pre_gate, post_gate, values, cotangent]
    lower = seq_index < quarters
    mixed = (pre_gate[0].astype(f32) * values[0]).astype(bf16)
    gated = (cotangent[0].astype(f32) * post_gate[0]).astype(bf16)
    a, b = jnp.where(lower, mixed, gated), jnp.where(lower, gated, mixed)
    store = pltpu.VMEM((quarters, BLOCK, width), bf16)
    short = jax.ShapeDtypeStruct((local * BLOCK + TAIL, BLOCK), bf16)
    message = jax.ShapeDtypeStruct((2 * local * BLOCK + TAIL, BLOCK), bf16)
    chunks = call(
        lambda *refs: pack_kernel(quarters, dp_count, *refs), "pack", place, pieces + [a, b],
        [short] * quarters + [message] * (quarters - 1) + [short], [pltpu.VMEM((quarters, local, BLOCK), f32)],
        flops=1000, nbytes=1000,
    )
    a_own, ab_own = chunks[:quarters], chunks[quarters:]
    r_in = [swap(a_own[j], quarters + j) for j in range(quarters)]
    ab_in = [ab_own[0]] + [swap(ab_own[j], j) for j in range(1, quarters - 1)]
    ab_in += [swap(a_own[-1], quarters - 1), swap(ab_own[-1], quarters - 1)]

    band = pltpu.VMEM((local, 2 * BLOCK, K), bf16)
    store = pltpu.VMEM((quarters, BLOCK, width), bf16)
    whole = pltpu.VMEM((parts, BLOCK, width), bf16)
    done = call(
        lambda *refs: sums_kernel(quarters, dp_count, *refs), "sums", place, ab_in + r_in, chunk_shapes(quarters, width, 2),
        [band, band, store, whole, store, store, pltpu.VMEM((owners, local, rows), f32)], flops=1000, nbytes=1000,
    )
    back = [done[0]] + [swap(done[j], j) for j in range(1, quarters)]
    token = lax.ppermute(done[0], "dp", [(i, i ^ 1) for i in range(dp_count)])
    (shares,) = call(
        lambda *refs: lags_kernel(quarters, *refs), "lags", place, ab_in + r_in,
        [jax.ShapeDtypeStruct((owners, BLOCK), f32)], [store, whole, pltpu.VMEM((local, K), f32)],
        flops=1000, nbytes=1000, after=[token],
    )
    arrived = lax.all_to_all(shares, every, 0, 0, tiled=True)

    early, last = list(range(quarters - 1)), [quarters - 1]
    outputs = gate_outputs(early, place, back, gates)
    output, grad_pre, grad_post, grad_values = gate_outputs(last, place, back, gates, outputs)
    total_tokens = dp_count * parts * pre_gate.shape[1] * (channels // groups)
    (mine,) = call(
        lambda *refs: owned_kernel(1.0 / float(total_tokens**0.5), *refs), "owned", place, [arrived],
        [jax.ShapeDtypeStruct((groups, rows), f32)], flops=1000, nbytes=1000,
    )
    return output, grad_pre, grad_post, grad_values, mine.T


def solution(mesh):
    def chosen(*shard):
        fits = swap_fits(*shard)
        return (swapped if fits else shards)(*shard)

    return jax.shard_map(
        chosen,
        mesh=mesh,
        in_specs=(
            P("dp", "seq", None),
            P("dp", "seq", None),
            P("dp", "seq", None),
            P("dp", "seq", None),
            P(("dp", "seq"), None),
        ),
        out_specs=(
            P("dp", "seq", None),
            P("dp", "seq", None),
            P("dp", "seq", None),
            P("dp", "seq", None),
            P(("dp", "seq"), None),
        ),
        check_vma=False,
    )
```

```python
import jax
import jax.numpy as jnp
import numpy as np
from jax import lax
from jax.experimental import pallas as pl
from jax.experimental.pallas import tpu as pltpu
from jax.sharding import PartitionSpec as P

K = 1024


def shifted(value, axis, steps):
    count = lax.axis_size(axis)
    first, last = (max(0, -steps), min(count, count - steps))
    return lax.ppermute(value, axis, [(source, source + steps) for source in range(first, last)])


def tile_index(lag_blocks, shard_len):
    offsets = np.arange(lag_blocks)[:, None, None] * shard_len
    rows_idx = np.arange(shard_len)[None, :, None]
    cols_idx = np.arange(shard_len)[None, None, :]
    return (offsets + rows_idx - cols_idx + shard_len).astype(np.int32)


def build_tiles(all_taps, lag_blocks, shard_len):
    tap_count = all_taps.shape[0]
    needed = (lag_blocks + 1) * shard_len
    trailing = max(needed - shard_len - tap_count, 0)
    padded = jnp.concatenate(
        [
            jnp.zeros((shard_len, all_taps.shape[1]), all_taps.dtype),
            all_taps,
            jnp.zeros((trailing, all_taps.shape[1]), all_taps.dtype),
        ],
        axis=0,
    )
    columns = padded.T
    return columns[:, tile_index(lag_blocks, shard_len)]


def earlier_relay(piece_in, history_len):

    def earlier_advance(moving, unused):
        arrived = shifted(moving, "seq", 1)
        return (arrived, arrived)

    unused_last, stacked = lax.scan(earlier_advance, piece_in, None, length=history_len)
    return jnp.concatenate([piece_in[None], stacked], axis=0)


def later_relay(piece_in, history_len):

    def later_advance(moving, unused):
        arrived = shifted(moving, "seq", -1)
        return (arrived, arrived)

    unused_last, stacked = lax.scan(later_advance, piece_in, None, length=history_len)
    return jnp.concatenate([piece_in[None], stacked], axis=0)


def lag_window(gated_rows, history, local_groups, group_width, lag_count):
    row_count = gated_rows.shape[0]
    span_len = history.shape[0]
    front_zero = jnp.zeros((row_count, history.shape[1]), history.dtype)
    widened = jnp.concatenate([front_zero, history], axis=0)
    gated_grp = gated_rows.reshape(row_count, local_groups, group_width).transpose(1, 0, 2)
    hist_grp = widened.reshape(span_len + row_count, local_groups, group_width).transpose(1, 0, 2)

    def one_group(pair_in):
        gated_one, hist_one = pair_in
        product = lax.dot_general(
            gated_one, hist_one, (((1,), (1,)), ((), ())), preferred_element_type=jnp.float32
        )
        padded = jnp.pad(product, ((0, 0), (0, row_count)))
        flat_line = jnp.concatenate(
            [padded.reshape(-1), jnp.zeros((row_count,), jnp.float32)], axis=0
        )
        skewed = flat_line.reshape(row_count, span_len + 2 * row_count + 1)
        diag_sums = jnp.sum(skewed, axis=0)
        return jnp.flip(diag_sums[1 : span_len + 1], axis=0)[:lag_count]

    return lax.map(one_group, (gated_grp, hist_grp))


def shards(pre_gate, post_gate, values, cotangent, filters):
    shard_len = pre_gate.shape[1]
    channels = pre_gate.shape[2]
    groups = filters.shape[1]
    group_size = channels // groups
    seq_count = lax.axis_size("seq")
    all_taps = lax.all_gather(filters, ("dp", "seq"), axis=0, tiled=True)
    mixed_in = (pre_gate[0].astype(jnp.float32) * values[0]).astype(jnp.bfloat16)
    gated = (cotangent[0].astype(jnp.float32) * post_gate[0]).astype(jnp.bfloat16)
    history_len = min(-(-K // shard_len), seq_count - 1)
    lag_blocks = history_len + 1
    mixed_ext = earlier_relay(mixed_in, history_len)
    gated_ext = later_relay(gated, history_len)
    mixed_four = mixed_ext.reshape(lag_blocks, shard_len, groups, group_size)
    gated_four = gated_ext.reshape(lag_blocks, shard_len, groups, group_size)
    tiles = build_tiles(all_taps, lag_blocks, shard_len)
    convolved = jnp.einsum(
        "gmij,mjgc->igc", tiles, mixed_four, preferred_element_type=jnp.float32
    ).reshape(shard_len, channels)
    carried = jnp.einsum(
        "gmji,mjgc->igc", tiles, gated_four, preferred_element_type=jnp.float32
    ).reshape(shard_len, channels)
    hist_len = lag_blocks * shard_len
    lag_count = min(K, hist_len)
    history = jnp.flip(mixed_ext, axis=0).reshape(hist_len, channels)
    lag_local = lag_window(gated, history, groups, group_size, lag_count)
    partial_grads = lag_local.T
    output = (post_gate[0].astype(jnp.float32) * convolved).astype(jnp.bfloat16)
    grad_post = (cotangent[0].astype(jnp.float32) * convolved).astype(jnp.bfloat16)
    grad_pre = (carried * values[0]).astype(jnp.bfloat16)
    grad_values = (carried * pre_gate[0]).astype(jnp.bfloat16)
    owned = lax.psum_scatter(partial_grads, ("dp", "seq"), scatter_dimension=0, tiled=True)
    total_tokens = lax.axis_size("dp") * shard_len * seq_count * group_size
    grad_filters = owned / float(total_tokens**0.5)
    return (output[None], grad_pre[None], grad_post[None], grad_values[None], grad_filters)


BLOCK = 128


def swap_fits(pre_gate, post_gate, values, cotangent, filters):
    parts, dp_count = lax.axis_size("seq"), lax.axis_size("dp")
    channels, groups = pre_gate.shape[2], filters.shape[1]
    return (
        parts >= 4
        and parts & (parts - 1) == 0
        and groups % parts == 0
        and channels // groups == BLOCK
        and pre_gate.shape[0] == 1
        and pre_gate.shape[1] == BLOCK
        and parts * BLOCK == K
        and filters.shape[0] * parts * dp_count == K
        and dp_count == parts // 2 == groups // (parts // 2)
    )


def swap(chunk, flip):
    count = lax.axis_size("seq")
    return lax.ppermute(chunk, "seq", [(i, i ^ flip) for i in range(count)])


def vmem_specs(count):
    return [pl.BlockSpec(memory_space=pltpu.VMEM)] * count


def chunk_shapes(count, width, blocks=1):
    return [jax.ShapeDtypeStruct((blocks * BLOCK, width), jnp.bfloat16)] * count


def call(kernel, name, place, operands, out_shape, scratch=(), flops=1000, nbytes=1000, after=()):
    def body(place_ref, *refs):
        kernel(place_ref, *refs[: len(operands)], *refs[len(operands) + len(after) :])

    return pl.pallas_call(
        body,
        in_specs=[pl.BlockSpec(memory_space=pltpu.SMEM)]
        + vmem_specs(len(operands))
        + [pl.BlockSpec(memory_space=pl.ANY)] * len(after),
        out_specs=vmem_specs(len(out_shape)),
        out_shape=out_shape,
        scratch_shapes=list(scratch),
        compiler_params=pltpu.CompilerParams(vmem_limit_bytes=20 * 1024 * 1024),
        cost_estimate=pl.CostEstimate(flops=flops, bytes_accessed=nbytes, transcendentals=0),
        name=name,
    )(place, *operands, *after)


TAIL = 16


def pack_kernel(quarters, pieces, place_ref, *refs):
    f32, bf16 = jnp.float32, jnp.bfloat16
    taps_in, (a_ref, b_ref), refs = refs[:pieces], refs[pieces : pieces + 2], refs[pieces + 2 :]
    a_outs, outs, (taps_ref,) = refs[:quarters], refs[quarters : 2 * quarters], refs[2 * quarters :]
    quarter = place_ref[1]
    local = taps_ref.shape[1]
    taps = jnp.concatenate([piece[...].astype(f32) for piece in taps_in], axis=1)
    for i in range(quarters):
        taps_ref[i] = taps[i * local : (i + 1) * local]
    for j in range(quarters):
        for g in range(local):
            columns = pl.ds(pl.multiple_of(((quarter ^ j) * local + g) * BLOCK, BLOCK), BLOCK)
            a = a_ref[:, columns]
            a_outs[j][g * BLOCK : (g + 1) * BLOCK] = a
            if j < quarters - 1:
                outs[j][g * BLOCK : (g + 1) * BLOCK] = a
                outs[j][(local + g) * BLOCK : (local + g + 1) * BLOCK] = b_ref[:, columns]
            else:
                outs[j][g * BLOCK : (g + 1) * BLOCK] = b_ref[:, columns]
        tail = jnp.concatenate([taps_ref[quarter ^ j], jnp.zeros((TAIL - local, BLOCK), f32)], axis=0).astype(bf16)
        a_outs[j][local * BLOCK :] = tail
        outs[j][-TAIL:] = tail


def bands(quarters, dp_count, place_ref, taps_in, taps_ref, causal_ref, anti_ref, causal_from, anti_to):
    half, quarter, dp_index = place_ref[0], place_ref[1], place_ref[2]
    for u in range(2):
        for j in range(quarters):
            tail = taps_in[u * quarters + j][-TAIL:].astype(jnp.float32)
            taps_ref[(half ^ u) * quarters + (quarter ^ j)] = tail[: taps_ref.shape[1]]
    rows = BLOCK // dp_count
    part = lax.broadcasted_iota(jnp.int32, (1, BLOCK), 1) // rows
    blocks = []
    for d in range(dp_count):
        way = lax.rem(dp_index + dp_count - d, dp_count)
        for h in range(2):
            block = None
            for q in range(quarters):
                shift = lax.rem(q + dp_count - way, dp_count) * rows
                moved = pltpu.roll(taps_ref[h * quarters + q], shift, 1)
                block = moved if block is None else jnp.where(part == q, moved, block)
            blocks.append(block)
    for g in range(causal_ref.shape[0]):
        line = jnp.concatenate([block[g : g + 1] for block in blocks] + [jnp.zeros((1, BLOCK), jnp.float32)], axis=1)
        shear = pltpu.roll(jnp.broadcast_to(line, (BLOCK, K + BLOCK)), 0, 1, stride=1, stride_axis=0)
        zero = jnp.zeros((BLOCK, BLOCK), jnp.bfloat16)
        count = K // BLOCK
        tiles = [shear[:, m * BLOCK : (m + 1) * BLOCK] for m in range(count)]
        for b in range(anti_to // BLOCK):
            columns = slice(b * BLOCK, (b + 1) * BLOCK)
            anti_ref[g, :BLOCK, columns] = tiles[b].astype(jnp.bfloat16)
            anti_ref[g, BLOCK:, columns] = tiles[b - 1].astype(jnp.bfloat16) if b else zero
        wanted = count - causal_from // BLOCK
        turned = [tile.T.astype(jnp.bfloat16) for tile in tiles[:wanted]] + [zero]
        for b in range(count - wanted, count):
            columns = slice(b * BLOCK, (b + 1) * BLOCK)
            causal_ref[g, :BLOCK, columns] = turned[count - 2 - b] if b < count - 1 else zero
            causal_ref[g, BLOCK:, columns] = turned[count - 1 - b]


def rows_of(ref, lanes):
    return ref[:, :, lanes].reshape(ref.shape[0] * BLOCK, BLOCK)


def dot(left, right):
    return jnp.dot(left, right, preferred_element_type=jnp.float32)


WIDE = 2 * BLOCK


def side_by_side(data):
    return jnp.concatenate([data[:-WIDE], data[WIDE:]], axis=1)


def causal_part(band, data):
    length = data.shape[0]
    both = dot(band[:, K - length + WIDE :], side_by_side(data))
    return both[:, :BLOCK], both[:, BLOCK:] + dot(band[:, K - length : K - length + WIDE], data[:WIDE])


def anti_part(band, data):
    length = data.shape[0]
    both = dot(band[:, : length - WIDE], side_by_side(data))
    return both[:, :BLOCK] + dot(band[:, length - WIDE : length], data[-WIDE:]), both[:, BLOCK:]


def lag_lines(mixed, mixed_first, gated, gated_first):
    count = mixed.shape[0] // BLOCK
    blocks = K // BLOCK
    still = [mixed[j * BLOCK : (j + 1) * BLOCK] for j in range(count)]
    ready = [gated[i * BLOCK : (i + 1) * BLOCK] for i in range(gated.shape[0] // BLOCK)]
    sums = [None] * blocks
    for lag in range(blocks):
        pairs = [(j, j + lag + mixed_first - gated_first) for j in range(count)]
        pairs = [(j, i) for j, i in pairs if 0 <= i < len(ready)]
        if pairs:
            left = jnp.concatenate([still[j] for j, _ in pairs], axis=1)
            right = jnp.concatenate([ready[i] for _, i in pairs], axis=1)
            sums[lag] = lax.dot_general(left, right, (((1,), (1,)), ((), ())), preferred_element_type=jnp.float32)
    last = max(m for m in range(blocks) if sums[m] is not None)
    zero = jnp.zeros((BLOCK, BLOCK), jnp.float32)
    table = jnp.concatenate([zero if term is None else term for term in sums[: last + 1]] + [zero], axis=1)
    span = (last + 2) * BLOCK
    parts, step = [table[row : row + 8] for row in range(0, BLOCK, 8)], 8
    while len(parts) > 1:
        parts = [near + pltpu.roll(far, span - step, 1) for near, far in zip(parts[::2], parts[1::2])]
        step *= 2
    total = parts[0]
    row = lax.broadcasted_iota(jnp.int32, (8, span), 0)
    for step in (1, 2, 4):
        total = jnp.where((row & step) != 0, pltpu.roll(total, span - step, 1), total)
    line = jnp.sum(total, axis=0, keepdims=True)[:, : span - BLOCK]
    if span - BLOCK < K:
        line = jnp.concatenate([line, jnp.zeros((1, K + BLOCK - span), jnp.float32)], axis=1)
    return line


def gather(quarters, place_ref, ab_in, r_in, a_ref, data_ref):
    half, quarter = place_ref[0], place_ref[1]
    local = a_ref.shape[2] // BLOCK
    for j in range(quarters):
        b_in, b_row = (ab_in[j], local) if j < quarters - 1 else (ab_in[j + 1], 0)
        for g in range(local):
            lanes = slice(g * BLOCK, (g + 1) * BLOCK)
            a_ref[quarter ^ j, :, lanes] = ab_in[j][g * BLOCK : (g + 1) * BLOCK]
            b_rows = slice((b_row + g) * BLOCK, (b_row + g + 1) * BLOCK)
            data_ref[half * quarters + (quarter ^ j), :, lanes] = b_in[b_rows]
            data_ref[(1 - half) * quarters + (quarter ^ j), :, lanes] = r_in[j][g * BLOCK : (g + 1) * BLOCK]


def lags_kernel(quarters, place_ref, *refs):
    ab_in, r_in, refs = refs[: quarters + 1], refs[quarters + 1 : 2 * quarters + 1], refs[2 * quarters + 1 :]
    shares_ref, a_ref, data_ref, lines_ref = refs
    gather(quarters, place_ref, ab_in, r_in, a_ref, data_ref)
    half = place_ref[0]
    local = lines_ref.shape[0]
    length = quarters * BLOCK

    @pl.when(half == 0)
    def lower():
        for g in range(local):
            lanes = slice(g * BLOCK, (g + 1) * BLOCK)
            mixed, gated = rows_of(a_ref, lanes), rows_of(data_ref, lanes)
            lines_ref[g : g + 1] = lag_lines(mixed, 0, gated if g < local // 2 else gated[:length], 0)

    @pl.when(half != 0)
    def upper():
        for g in range(local):
            lanes = slice(g * BLOCK, (g + 1) * BLOCK)
            gated, mixed = rows_of(a_ref, lanes), rows_of(data_ref, lanes)
            first = quarters if g < local // 2 else 0
            lines_ref[g : g + 1] = lag_lines(mixed[first * BLOCK :], first, gated, quarters)

    step = BLOCK // local
    lane = lax.broadcasted_iota(jnp.int32, (1, K), 1) % BLOCK // step
    lines = lines_ref[...]
    moved = {d: pltpu.roll(lines, d * step % K, 1) if d else lines for d in range(1 - local, local)}
    for u in range(local):
        row = moved[-u][:1]
        for g in range(1, local):
            row = jnp.where(lane == g, moved[g - u][g : g + 1], row)
        for block in range(K // BLOCK):
            shares_ref[block * local + u : block * local + u + 1] = row[:, block * BLOCK : (block + 1) * BLOCK]


def sums_kernel(quarters, dp_count, place_ref, *refs):
    ab_in, r_in, refs = refs[: quarters + 1], refs[quarters + 1 : 2 * quarters + 1], refs[2 * quarters + 1 :]
    outs, refs = refs[:quarters], refs[quarters:]
    causal_ref, anti_ref, a_ref, data_ref, done_ref, taps_ref = refs
    gather(quarters, place_ref, ab_in, r_in, a_ref, data_ref)
    tails = ab_in[:quarters] + r_in
    half, quarter = place_ref[0], place_ref[1]
    local = causal_ref.shape[0]

    def work(a_part, a_band, b_part, b_band):
        for g in range(local):
            lanes = slice(g * BLOCK, (g + 1) * BLOCK)
            for rows, sums in (
                (slice(0, BLOCK), a_part(a_band.at[g], rows_of(a_ref, lanes))),
                (slice(BLOCK, WIDE), b_part(b_band.at[g], rows_of(data_ref, lanes))),
            ):
                for p in range(2):
                    done_ref[2 * p : 2 * p + 2, g, rows] = sums[p].reshape(2, BLOCK, BLOCK).astype(jnp.bfloat16)

    @pl.when(half == 0)
    def lower():
        bands(quarters, dp_count, place_ref, tails, taps_ref, causal_ref, anti_ref, K // 2, K)
        work(causal_part, causal_ref, anti_part, anti_ref)

    @pl.when(half != 0)
    def upper():
        bands(quarters, dp_count, place_ref, tails, taps_ref, causal_ref, anti_ref, 0, K // 2)
        work(anti_part, anti_ref, causal_part, causal_ref)

    for j in range(quarters):
        outs[j][...] = done_ref[quarter ^ j].reshape(local * WIDE, BLOCK)


def owned_kernel(scale, place_ref, arrived_ref, out_ref):
    groups, rows = out_ref.shape
    local = BLOCK // rows
    quarters = groups // local
    total = arrived_ref[:quarters]
    for i in range(1, arrived_ref.shape[0] // quarters):
        total = total + arrived_ref[i * quarters : (i + 1) * quarters]
    total = total * scale
    for g in range(local):
        part = (total if g == 0 else pltpu.roll(total, BLOCK - g * rows, 1))[:, :rows]
        for q in range(quarters):
            out_ref[q * local + g : q * local + g + 1] = part[q : q + 1]


def outputs_kernel(js, place_ref, *refs):
    f32, bf16 = jnp.float32, jnp.bfloat16
    count = len(js)
    back, inputs = refs[:count], refs[count : count + 4]
    outputs, results, sem = refs[-9:-5], refs[-5:-1], refs[-1]
    half, quarter = place_ref[0], place_ref[1]
    width = results[0].shape[2]

    def copies(i):
        columns = pl.ds(pl.multiple_of((quarter ^ js[i]) * width, width), width)
        return [
            pltpu.make_async_copy(store.at[i], target.at[0, :, columns], sem.at[i, k])
            for k, (store, target) in enumerate(zip(results, outputs))
        ]

    for i in range(count):
        for g in range(width // BLOCK):
            lanes = slice(g * BLOCK, (g + 1) * BLOCK)
            columns = pl.ds(pl.multiple_of((quarter ^ js[i]) * width + g * BLOCK, BLOCK), BLOCK)
            pre, post, values, cot = [source[0, :, columns].astype(f32) for source in inputs]
            sums = back[i][g * WIDE : (g + 1) * WIDE].astype(f32)
            a_sum, b_sum = sums[:BLOCK], sums[BLOCK:]
            convolved, carried = jnp.where(half == 0, a_sum, b_sum), jnp.where(half == 0, b_sum, a_sum)
            for result, value in zip(results, (post * convolved, carried * values, cot * convolved, carried * pre)):
                result[i, :, lanes] = value.astype(bf16)
        for copy in copies(i):
            copy.start()
    for i in range(count):
        for copy in copies(i):
            copy.wait()


def gate_outputs(js, place, back, gates, earlier=()):
    hbm = [pl.BlockSpec(memory_space=pltpu.HBM)] * 4
    store = pltpu.VMEM((len(js), BLOCK, back[0].shape[0] // 2), jnp.bfloat16)
    return pl.pallas_call(
        lambda *refs: outputs_kernel(js, *refs),
        in_specs=[pl.BlockSpec(memory_space=pltpu.SMEM)] + vmem_specs(len(js) + 4) + hbm[: len(earlier)],
        out_specs=hbm,
        out_shape=[jax.ShapeDtypeStruct(gates[0].shape, jnp.bfloat16)] * 4,
        input_output_aliases={1 + len(js) + 4 + k: k for k in range(len(earlier))},
        scratch_shapes=[store] * 4 + [pltpu.SemaphoreType.DMA((len(js), 4))],
        compiler_params=pltpu.CompilerParams(vmem_limit_bytes=20 * 1024 * 1024),
        cost_estimate=pl.CostEstimate(flops=1000, bytes_accessed=1000, transcendentals=0),
        name="outputs",
    )(place, *[back[j] for j in js], *gates, *earlier)


def swapped(pre_gate, post_gate, values, cotangent, filters):
    parts, dp_count = lax.axis_size("seq"), lax.axis_size("dp")
    quarters = parts // 2
    channels, groups = pre_gate.shape[2], filters.shape[1]
    width, local = channels // quarters, groups // quarters
    seq_index = lax.axis_index("seq")
    place = jnp.stack([seq_index // quarters, seq_index % quarters, lax.axis_index("dp")]).astype(jnp.int32)
    owners = parts * dp_count
    rows = filters.shape[0]
    f32, bf16 = jnp.float32, jnp.bfloat16
    every = ("dp", "seq")

    taps = filters.T
    pieces = [taps]
    for p in range(1, dp_count):
        pieces.append(lax.ppermute(taps, "dp", [(i, (i + p) % dp_count) for i in range(dp_count)]))

    gates = [pre_gate, post_gate, values, cotangent]
    lower = seq_index < quarters
    mixed = (pre_gate[0].astype(f32) * values[0]).astype(bf16)
    gated = (cotangent[0].astype(f32) * post_gate[0]).astype(bf16)
    a, b = jnp.where(lower, mixed, gated), jnp.where(lower, gated, mixed)
    store = pltpu.VMEM((quarters, BLOCK, width), bf16)
    short = jax.ShapeDtypeStruct((local * BLOCK + TAIL, BLOCK), bf16)
    message = jax.ShapeDtypeStruct((2 * local * BLOCK + TAIL, BLOCK), bf16)
    chunks = call(
        lambda *refs: pack_kernel(quarters, dp_count, *refs), "pack", place, pieces + [a, b],
        [short] * quarters + [message] * (quarters - 1) + [short], [pltpu.VMEM((quarters, local, BLOCK), f32)],
        flops=1000, nbytes=1000,
    )
    a_own, ab_own = chunks[:quarters], chunks[quarters:]
    r_in = [swap(a_own[j], quarters + j) for j in range(quarters)]
    ab_in = [ab_own[0]] + [swap(ab_own[j], j) for j in range(1, quarters - 1)]
    ab_in += [swap(a_own[-1], quarters - 1), swap(ab_own[-1], quarters - 1)]

    band = pltpu.VMEM((local, 2 * BLOCK, K), bf16)
    store = pltpu.VMEM((quarters, BLOCK, width), bf16)
    whole = pltpu.VMEM((parts, BLOCK, width), bf16)
    done = pl.pallas_call(
        lambda *refs: sums_kernel(quarters, dp_count, *refs),
        in_specs=[pl.BlockSpec(memory_space=pltpu.SMEM)] + vmem_specs(2 * quarters + 1),
        out_specs=vmem_specs(quarters),
        out_shape=[jax.ShapeDtypeStruct((2 * local * BLOCK, BLOCK), bf16)] * quarters,
        scratch_shapes=[
            band, band, store, whole, pltpu.VMEM((quarters, local, WIDE, BLOCK), bf16),
            pltpu.VMEM((parts, 8, BLOCK), f32),
        ],
        compiler_params=pltpu.CompilerParams(vmem_limit_bytes=20 * 1024 * 1024),
        cost_estimate=pl.CostEstimate(flops=1000, bytes_accessed=1000, transcendentals=0),
        name="sums",
    )(place, *ab_in, *r_in)
    back = [done[0]] + [swap(done[j], j) for j in range(1, quarters)]
    token = lax.ppermute(done[0], "dp", [(i, i ^ 1) for i in range(dp_count)])
    (shares,) = call(
        lambda *refs: lags_kernel(quarters, *refs), "lags", place, ab_in + r_in,
        [jax.ShapeDtypeStruct((owners, BLOCK), f32)], [store, whole, pltpu.VMEM((local, K), f32)],
        flops=1000, nbytes=1000, after=[token],
    )
    arrived = lax.all_to_all(shares, every, 0, 0, tiled=True)

    early, last = [0, quarters - 1], list(range(1, quarters - 1))
    outputs = gate_outputs(early, place, back, gates)
    output, grad_pre, grad_post, grad_values = gate_outputs(last, place, back, gates, outputs)
    total_tokens = dp_count * parts * pre_gate.shape[1] * (channels // groups)
    (mine,) = call(
        lambda *refs: owned_kernel(1.0 / float(total_tokens**0.5), *refs), "owned", place, [arrived],
        [jax.ShapeDtypeStruct((groups, rows), f32)], flops=1000, nbytes=1000,
    )
    return output, grad_pre, grad_post, grad_values, mine.T


def solution(mesh):
    def chosen(*shard):
        fits = swap_fits(*shard)
        return (swapped if fits else shards)(*shard)

    return jax.shard_map(
        chosen,
        mesh=mesh,
        in_specs=(
            P("dp", "seq", None),
            P("dp", "seq", None),
            P("dp", "seq", None),
            P("dp", "seq", None),
            P(("dp", "seq"), None),
        ),
        out_specs=(
            P("dp", "seq", None),
            P("dp", "seq", None),
            P("dp", "seq", None),
            P("dp", "seq", None),
            P(("dp", "seq"), None),
        ),
        check_vma=False,
    )
```

```python
import jax
import jax.numpy as jnp
import numpy as np
from jax import lax
from jax.experimental import pallas as pl
from jax.experimental.pallas import tpu as pltpu
from jax.sharding import PartitionSpec as P

K = 1024


def shifted(value, axis, steps):
    count = lax.axis_size(axis)
    first, last = (max(0, -steps), min(count, count - steps))
    return lax.ppermute(value, axis, [(source, source + steps) for source in range(first, last)])


def tile_index(lag_blocks, shard_len):
    offsets = np.arange(lag_blocks)[:, None, None] * shard_len
    rows_idx = np.arange(shard_len)[None, :, None]
    cols_idx = np.arange(shard_len)[None, None, :]
    return (offsets + rows_idx - cols_idx + shard_len).astype(np.int32)


def build_tiles(all_taps, lag_blocks, shard_len):
    tap_count = all_taps.shape[0]
    needed = (lag_blocks + 1) * shard_len
    trailing = max(needed - shard_len - tap_count, 0)
    padded = jnp.concatenate(
        [
            jnp.zeros((shard_len, all_taps.shape[1]), all_taps.dtype),
            all_taps,
            jnp.zeros((trailing, all_taps.shape[1]), all_taps.dtype),
        ],
        axis=0,
    )
    columns = padded.T
    return columns[:, tile_index(lag_blocks, shard_len)]


def earlier_relay(piece_in, history_len):

    def earlier_advance(moving, unused):
        arrived = shifted(moving, "seq", 1)
        return (arrived, arrived)

    unused_last, stacked = lax.scan(earlier_advance, piece_in, None, length=history_len)
    return jnp.concatenate([piece_in[None], stacked], axis=0)


def later_relay(piece_in, history_len):

    def later_advance(moving, unused):
        arrived = shifted(moving, "seq", -1)
        return (arrived, arrived)

    unused_last, stacked = lax.scan(later_advance, piece_in, None, length=history_len)
    return jnp.concatenate([piece_in[None], stacked], axis=0)


def lag_window(gated_rows, history, local_groups, group_width, lag_count):
    row_count = gated_rows.shape[0]
    span_len = history.shape[0]
    front_zero = jnp.zeros((row_count, history.shape[1]), history.dtype)
    widened = jnp.concatenate([front_zero, history], axis=0)
    gated_grp = gated_rows.reshape(row_count, local_groups, group_width).transpose(1, 0, 2)
    hist_grp = widened.reshape(span_len + row_count, local_groups, group_width).transpose(1, 0, 2)

    def one_group(pair_in):
        gated_one, hist_one = pair_in
        product = lax.dot_general(
            gated_one, hist_one, (((1,), (1,)), ((), ())), preferred_element_type=jnp.float32
        )
        padded = jnp.pad(product, ((0, 0), (0, row_count)))
        flat_line = jnp.concatenate(
            [padded.reshape(-1), jnp.zeros((row_count,), jnp.float32)], axis=0
        )
        skewed = flat_line.reshape(row_count, span_len + 2 * row_count + 1)
        diag_sums = jnp.sum(skewed, axis=0)
        return jnp.flip(diag_sums[1 : span_len + 1], axis=0)[:lag_count]

    return lax.map(one_group, (gated_grp, hist_grp))


def shards(pre_gate, post_gate, values, cotangent, filters):
    shard_len = pre_gate.shape[1]
    channels = pre_gate.shape[2]
    groups = filters.shape[1]
    group_size = channels // groups
    seq_count = lax.axis_size("seq")
    all_taps = lax.all_gather(filters, ("dp", "seq"), axis=0, tiled=True)
    mixed_in = (pre_gate[0].astype(jnp.float32) * values[0]).astype(jnp.bfloat16)
    gated = (cotangent[0].astype(jnp.float32) * post_gate[0]).astype(jnp.bfloat16)
    history_len = min(-(-K // shard_len), seq_count - 1)
    lag_blocks = history_len + 1
    mixed_ext = earlier_relay(mixed_in, history_len)
    gated_ext = later_relay(gated, history_len)
    mixed_four = mixed_ext.reshape(lag_blocks, shard_len, groups, group_size)
    gated_four = gated_ext.reshape(lag_blocks, shard_len, groups, group_size)
    tiles = build_tiles(all_taps, lag_blocks, shard_len)
    convolved = jnp.einsum(
        "gmij,mjgc->igc", tiles, mixed_four, preferred_element_type=jnp.float32
    ).reshape(shard_len, channels)
    carried = jnp.einsum(
        "gmji,mjgc->igc", tiles, gated_four, preferred_element_type=jnp.float32
    ).reshape(shard_len, channels)
    hist_len = lag_blocks * shard_len
    lag_count = min(K, hist_len)
    history = jnp.flip(mixed_ext, axis=0).reshape(hist_len, channels)
    lag_local = lag_window(gated, history, groups, group_size, lag_count)
    partial_grads = lag_local.T
    output = (post_gate[0].astype(jnp.float32) * convolved).astype(jnp.bfloat16)
    grad_post = (cotangent[0].astype(jnp.float32) * convolved).astype(jnp.bfloat16)
    grad_pre = (carried * values[0]).astype(jnp.bfloat16)
    grad_values = (carried * pre_gate[0]).astype(jnp.bfloat16)
    owned = lax.psum_scatter(partial_grads, ("dp", "seq"), scatter_dimension=0, tiled=True)
    total_tokens = lax.axis_size("dp") * shard_len * seq_count * group_size
    grad_filters = owned / float(total_tokens**0.5)
    return (output[None], grad_pre[None], grad_post[None], grad_values[None], grad_filters)


BLOCK = 128


def swap_fits(pre_gate, post_gate, values, cotangent, filters):
    parts, dp_count = lax.axis_size("seq"), lax.axis_size("dp")
    channels, groups = pre_gate.shape[2], filters.shape[1]
    return (
        parts >= 4
        and parts & (parts - 1) == 0
        and groups % parts == 0
        and channels // groups == BLOCK
        and pre_gate.shape[0] == 1
        and pre_gate.shape[1] == BLOCK
        and parts * BLOCK == K
        and filters.shape[0] * parts * dp_count == K
        and dp_count == parts // 2 == groups // (parts // 2)
    )


def swap(chunk, flip):
    count = lax.axis_size("seq")
    return lax.ppermute(chunk, "seq", [(i, i ^ flip) for i in range(count)])


def vmem_specs(count):
    return [pl.BlockSpec(memory_space=pltpu.VMEM)] * count


def chunk_shapes(count, width, blocks=1):
    return [jax.ShapeDtypeStruct((blocks * BLOCK, width), jnp.bfloat16)] * count


def call(kernel, name, place, operands, out_shape, scratch=(), flops=1000, nbytes=1000, after=()):
    def body(place_ref, *refs):
        kernel(place_ref, *refs[: len(operands)], *refs[len(operands) + len(after) :])

    return pl.pallas_call(
        body,
        in_specs=[pl.BlockSpec(memory_space=pltpu.SMEM)]
        + vmem_specs(len(operands))
        + [pl.BlockSpec(memory_space=pl.ANY)] * len(after),
        out_specs=vmem_specs(len(out_shape)),
        out_shape=out_shape,
        scratch_shapes=list(scratch),
        compiler_params=pltpu.CompilerParams(vmem_limit_bytes=20 * 1024 * 1024),
        cost_estimate=pl.CostEstimate(flops=flops, bytes_accessed=nbytes, transcendentals=0),
        name=name,
    )(place, *operands, *after)


TAIL = 16


def pack_kernel(quarters, pieces, place_ref, *refs):
    f32, bf16 = jnp.float32, jnp.bfloat16
    taps_in, (a_ref, b_ref), refs = refs[:pieces], refs[pieces : pieces + 2], refs[pieces + 2 :]
    a_outs, outs, (taps_ref,) = refs[:quarters], refs[quarters : 2 * quarters], refs[2 * quarters :]
    quarter = place_ref[1]
    local = taps_ref.shape[1]
    taps = jnp.concatenate([piece[...].astype(f32) for piece in taps_in], axis=1)
    for i in range(quarters):
        taps_ref[i] = taps[i * local : (i + 1) * local]
    for j in range(quarters):
        for g in range(local):
            columns = pl.ds(pl.multiple_of(((quarter ^ j) * local + g) * BLOCK, BLOCK), BLOCK)
            a = a_ref[:, columns]
            a_outs[j][g * BLOCK : (g + 1) * BLOCK] = a
            if j < quarters - 1:
                outs[j][g * BLOCK : (g + 1) * BLOCK] = a
                outs[j][(local + g) * BLOCK : (local + g + 1) * BLOCK] = b_ref[:, columns]
            else:
                outs[j][g * BLOCK : (g + 1) * BLOCK] = b_ref[:, columns]
        tail = jnp.concatenate([taps_ref[quarter ^ j], jnp.zeros((TAIL - local, BLOCK), f32)], axis=0).astype(bf16)
        a_outs[j][local * BLOCK :] = tail
        outs[j][-TAIL:] = tail


def bands(quarters, dp_count, place_ref, taps_in, taps_ref, causal_ref, anti_ref, causal_from, anti_to):
    half, quarter, dp_index = place_ref[0], place_ref[1], place_ref[2]
    for u in range(2):
        for j in range(quarters):
            tail = taps_in[u * quarters + j][-TAIL:].astype(jnp.float32)
            taps_ref[(half ^ u) * quarters + (quarter ^ j)] = tail[: taps_ref.shape[1]]
    rows = BLOCK // dp_count
    part = lax.broadcasted_iota(jnp.int32, (1, BLOCK), 1) // rows
    blocks = []
    for d in range(dp_count):
        way = dp_index ^ d
        for h in range(2):
            block = None
            for q in range(quarters):
                shift = lax.rem(q + dp_count - way, dp_count) * rows
                moved = pltpu.roll(taps_ref[h * quarters + q], shift, 1)
                block = moved if block is None else jnp.where(part == q, moved, block)
            blocks.append(block)
    for g in range(causal_ref.shape[0]):
        line = jnp.concatenate([block[g : g + 1] for block in blocks] + [jnp.zeros((1, BLOCK), jnp.float32)], axis=1)
        shear = pltpu.roll(jnp.broadcast_to(line, (BLOCK, K + BLOCK)), 0, 1, stride=1, stride_axis=0)
        zero = jnp.zeros((BLOCK, BLOCK), jnp.bfloat16)
        count = K // BLOCK
        tiles = [shear[:, m * BLOCK : (m + 1) * BLOCK] for m in range(count)]
        for b in range(anti_to // BLOCK):
            columns = slice(b * BLOCK, (b + 1) * BLOCK)
            anti_ref[g, :BLOCK, columns] = tiles[b].astype(jnp.bfloat16)
            anti_ref[g, BLOCK:, columns] = tiles[b - 1].astype(jnp.bfloat16) if b else zero
        wanted = count - causal_from // BLOCK
        turned = [tile.T.astype(jnp.bfloat16) for tile in tiles[:wanted]] + [zero]
        for b in range(count - wanted, count):
            columns = slice(b * BLOCK, (b + 1) * BLOCK)
            causal_ref[g, :BLOCK, columns] = turned[count - 2 - b] if b < count - 1 else zero
            causal_ref[g, BLOCK:, columns] = turned[count - 1 - b]


def rows_of(ref, lanes):
    return ref[:, :, lanes].reshape(ref.shape[0] * BLOCK, BLOCK)


def dot(left, right):
    return jnp.dot(left, right, preferred_element_type=jnp.float32)


WIDE = 2 * BLOCK


def side_by_side(data):
    return jnp.concatenate([data[:-WIDE], data[WIDE:]], axis=1)


def causal_part(band, data):
    length = data.shape[0]
    both = dot(band[:, K - length + WIDE :], side_by_side(data))
    return both[:, :BLOCK], both[:, BLOCK:] + dot(band[:, K - length : K - length + WIDE], data[:WIDE])


def anti_part(band, data):
    length = data.shape[0]
    both = dot(band[:, : length - WIDE], side_by_side(data))
    return both[:, :BLOCK] + dot(band[:, length - WIDE : length], data[-WIDE:]), both[:, BLOCK:]


def lag_lines(mixed, mixed_first, gated, gated_first):
    count = mixed.shape[0] // BLOCK
    blocks = K // BLOCK
    still = [mixed[j * BLOCK : (j + 1) * BLOCK] for j in range(count)]
    ready = [gated[i * BLOCK : (i + 1) * BLOCK] for i in range(gated.shape[0] // BLOCK)]
    sums = [None] * blocks
    for lag in range(blocks):
        pairs = [(j, j + lag + mixed_first - gated_first) for j in range(count)]
        pairs = [(j, i) for j, i in pairs if 0 <= i < len(ready)]
        if pairs:
            left = jnp.concatenate([still[j] for j, _ in pairs], axis=1)
            right = jnp.concatenate([ready[i] for _, i in pairs], axis=1)
            sums[lag] = lax.dot_general(left, right, (((1,), (1,)), ((), ())), preferred_element_type=jnp.float32)
    last = max(m for m in range(blocks) if sums[m] is not None)
    zero = jnp.zeros((BLOCK, BLOCK), jnp.float32)
    table = jnp.concatenate([zero if term is None else term for term in sums[: last + 1]] + [zero], axis=1)
    span = (last + 2) * BLOCK
    parts, step = [table[row : row + 8] for row in range(0, BLOCK, 8)], 8
    while len(parts) > 1:
        parts = [near + pltpu.roll(far, span - step, 1) for near, far in zip(parts[::2], parts[1::2])]
        step *= 2
    total = parts[0]
    row = lax.broadcasted_iota(jnp.int32, (8, span), 0)
    for step in (1, 2, 4):
        total = jnp.where((row & step) != 0, pltpu.roll(total, span - step, 1), total)
    line = jnp.sum(total, axis=0, keepdims=True)[:, : span - BLOCK]
    if span - BLOCK < K:
        line = jnp.concatenate([line, jnp.zeros((1, K + BLOCK - span), jnp.float32)], axis=1)
    return line


def gather(quarters, place_ref, ab_in, r_in, a_ref, data_ref):
    half, quarter = place_ref[0], place_ref[1]
    local = a_ref.shape[2] // BLOCK
    for j in range(quarters):
        b_in, b_row = (ab_in[j], local) if j < quarters - 1 else (ab_in[j + 1], 0)
        for g in range(local):
            lanes = slice(g * BLOCK, (g + 1) * BLOCK)
            a_ref[quarter ^ j, :, lanes] = ab_in[j][g * BLOCK : (g + 1) * BLOCK]
            b_rows = slice((b_row + g) * BLOCK, (b_row + g + 1) * BLOCK)
            data_ref[half * quarters + (quarter ^ j), :, lanes] = b_in[b_rows]
            data_ref[(1 - half) * quarters + (quarter ^ j), :, lanes] = r_in[j][g * BLOCK : (g + 1) * BLOCK]


def lags_kernel(quarters, place_ref, *refs):
    ab_in, r_in, refs = refs[: quarters + 1], refs[quarters + 1 : 2 * quarters + 1], refs[2 * quarters + 1 :]
    shares_ref, a_ref, data_ref, lines_ref = refs
    gather(quarters, place_ref, ab_in, r_in, a_ref, data_ref)
    half = place_ref[0]
    local = lines_ref.shape[0]
    length = quarters * BLOCK

    @pl.when(half == 0)
    def lower():
        for g in range(local):
            lanes = slice(g * BLOCK, (g + 1) * BLOCK)
            mixed, gated = rows_of(a_ref, lanes), rows_of(data_ref, lanes)
            lines_ref[g : g + 1] = lag_lines(mixed, 0, gated if g < local // 2 else gated[:length], 0)

    @pl.when(half != 0)
    def upper():
        for g in range(local):
            lanes = slice(g * BLOCK, (g + 1) * BLOCK)
            gated, mixed = rows_of(a_ref, lanes), rows_of(data_ref, lanes)
            first = quarters if g < local // 2 else 0
            lines_ref[g : g + 1] = lag_lines(mixed[first * BLOCK :], first, gated, quarters)

    step = BLOCK // local
    owners = shares_ref.shape[0]
    for block in range(K // BLOCK):
        shares_ref[block * local : (block + 1) * local] = lines_ref[:, block * BLOCK : (block + 1) * BLOCK]
    rows = shares_ref[...]
    way = lax.broadcasted_iota(jnp.int32, rows.shape, 1) // step - lax.broadcasted_iota(jnp.int32, rows.shape, 0) % local
    sorted_rows = rows
    for d in range(1 - local, local):
        if d:
            moved = pltpu.roll(pltpu.roll(rows, -d % owners, 0), d * step % BLOCK, 1)
            sorted_rows = jnp.where(way == d, moved, sorted_rows)
    shares_ref[...] = sorted_rows


def sums_kernel(quarters, dp_count, place_ref, *refs):
    ab_in, r_in, refs = refs[: quarters + 1], refs[quarters + 1 : 2 * quarters + 1], refs[2 * quarters + 1 :]
    outs, refs = refs[:quarters], refs[quarters:]
    causal_ref, anti_ref, a_ref, data_ref, done_ref, taps_ref = refs
    gather(quarters, place_ref, ab_in, r_in, a_ref, data_ref)
    tails = ab_in[:quarters] + r_in
    half, quarter = place_ref[0], place_ref[1]
    local = causal_ref.shape[0]

    def work(a_part, a_band, b_part, b_band):
        for g in range(local):
            lanes = slice(g * BLOCK, (g + 1) * BLOCK)
            for rows, sums in (
                (slice(0, BLOCK), a_part(a_band.at[g], rows_of(a_ref, lanes))),
                (slice(BLOCK, WIDE), b_part(b_band.at[g], rows_of(data_ref, lanes))),
            ):
                for p in range(2):
                    done_ref[2 * p : 2 * p + 2, g, rows] = sums[p].reshape(2, BLOCK, BLOCK).astype(jnp.bfloat16)

    @pl.when(half == 0)
    def lower():
        bands(quarters, dp_count, place_ref, tails, taps_ref, causal_ref, anti_ref, K // 2, K)
        work(causal_part, causal_ref, anti_part, anti_ref)

    @pl.when(half != 0)
    def upper():
        bands(quarters, dp_count, place_ref, tails, taps_ref, causal_ref, anti_ref, 0, K // 2)
        work(anti_part, anti_ref, causal_part, causal_ref)

    for j in range(quarters):
        outs[j][...] = done_ref[quarter ^ j].reshape(local * WIDE, BLOCK)


def owned_kernel(scale, place_ref, arrived_ref, out_ref):
    groups, rows = out_ref.shape
    local = BLOCK // rows
    quarters = groups // local
    total = arrived_ref[:quarters]
    for i in range(1, arrived_ref.shape[0] // quarters):
        total = total + arrived_ref[i * quarters : (i + 1) * quarters]
    total = total * scale
    for g in range(local):
        part = (total if g == 0 else pltpu.roll(total, BLOCK - g * rows, 1))[:, :rows]
        for q in range(quarters):
            out_ref[q * local + g : q * local + g + 1] = part[q : q + 1]


def outputs_kernel(js, place_ref, *refs):
    f32, bf16 = jnp.float32, jnp.bfloat16
    count = len(js)
    back, inputs = refs[:count], refs[count : count + 4]
    outputs, results, sem = refs[-9:-5], refs[-5:-1], refs[-1]
    half, quarter = place_ref[0], place_ref[1]
    width = results[0].shape[2]

    def copies(i):
        columns = pl.ds(pl.multiple_of((quarter ^ js[i]) * width, width), width)
        return [
            pltpu.make_async_copy(store.at[i], target.at[0, :, columns], sem.at[i, k])
            for k, (store, target) in enumerate(zip(results, outputs))
        ]

    for i in range(count):
        for g in range(width // BLOCK):
            lanes = slice(g * BLOCK, (g + 1) * BLOCK)
            columns = pl.ds(pl.multiple_of((quarter ^ js[i]) * width + g * BLOCK, BLOCK), BLOCK)
            pre, post, values, cot = [source[0, :, columns].astype(f32) for source in inputs]
            sums = back[i][g * WIDE : (g + 1) * WIDE].astype(f32)
            a_sum, b_sum = sums[:BLOCK], sums[BLOCK:]
            convolved, carried = jnp.where(half == 0, a_sum, b_sum), jnp.where(half == 0, b_sum, a_sum)
            for result, value in zip(results, (post * convolved, carried * values, cot * convolved, carried * pre)):
                result[i, :, lanes] = value.astype(bf16)
        for copy in copies(i):
            copy.start()
    for i in range(count):
        for copy in copies(i):
            copy.wait()


def gate_outputs(js, place, back, gates, earlier=()):
    hbm = [pl.BlockSpec(memory_space=pltpu.HBM)] * 4
    store = pltpu.VMEM((len(js), BLOCK, back[0].shape[0] // 2), jnp.bfloat16)
    return pl.pallas_call(
        lambda *refs: outputs_kernel(js, *refs),
        in_specs=[pl.BlockSpec(memory_space=pltpu.SMEM)] + vmem_specs(len(js) + 4) + hbm[: len(earlier)],
        out_specs=hbm,
        out_shape=[jax.ShapeDtypeStruct(gates[0].shape, jnp.bfloat16)] * 4,
        input_output_aliases={1 + len(js) + 4 + k: k for k in range(len(earlier))},
        scratch_shapes=[store] * 4 + [pltpu.SemaphoreType.DMA((len(js), 4))],
        compiler_params=pltpu.CompilerParams(vmem_limit_bytes=20 * 1024 * 1024),
        cost_estimate=pl.CostEstimate(flops=1000, bytes_accessed=1000, transcendentals=0),
        name="outputs",
    )(place, *[back[j] for j in js], *gates, *earlier)


def swapped(pre_gate, post_gate, values, cotangent, filters):
    parts, dp_count = lax.axis_size("seq"), lax.axis_size("dp")
    quarters = parts // 2
    channels, groups = pre_gate.shape[2], filters.shape[1]
    width, local = channels // quarters, groups // quarters
    seq_index = lax.axis_index("seq")
    place = jnp.stack([seq_index // quarters, seq_index % quarters, lax.axis_index("dp")]).astype(jnp.int32)
    owners = parts * dp_count
    rows = filters.shape[0]
    f32, bf16 = jnp.float32, jnp.bfloat16
    every = ("dp", "seq")

    taps = filters.T
    pieces = [taps]
    for p in range(1, dp_count):
        pieces.append(lax.ppermute(taps, "dp", [(i, i ^ p) for i in range(dp_count)]))

    gates = [pre_gate, post_gate, values, cotangent]
    lower = seq_index < quarters
    mixed = (pre_gate[0].astype(f32) * values[0]).astype(bf16)
    gated = (cotangent[0].astype(f32) * post_gate[0]).astype(bf16)
    a, b = jnp.where(lower, mixed, gated), jnp.where(lower, gated, mixed)
    store = pltpu.VMEM((quarters, BLOCK, width), bf16)
    short = jax.ShapeDtypeStruct((local * BLOCK + TAIL, BLOCK), bf16)
    message = jax.ShapeDtypeStruct((2 * local * BLOCK + TAIL, BLOCK), bf16)
    chunks = call(
        lambda *refs: pack_kernel(quarters, dp_count, *refs), "pack", place, pieces + [a, b],
        [short] * quarters + [message] * (quarters - 1) + [short], [pltpu.VMEM((quarters, local, BLOCK), f32)],
        flops=1000, nbytes=1000,
    )
    a_own, ab_own = chunks[:quarters], chunks[quarters:]
    r_in = [swap(a_own[j], quarters + j) for j in range(quarters)]
    ab_in = [ab_own[0]] + [swap(ab_own[j], j) for j in range(1, quarters - 1)]
    ab_in += [swap(a_own[-1], quarters - 1), swap(ab_own[-1], quarters - 1)]

    band = pltpu.VMEM((local, 2 * BLOCK, K), bf16)
    store = pltpu.VMEM((quarters, BLOCK, width), bf16)
    whole = pltpu.VMEM((parts, BLOCK, width), bf16)
    done = pl.pallas_call(
        lambda *refs: sums_kernel(quarters, dp_count, *refs),
        in_specs=[pl.BlockSpec(memory_space=pltpu.SMEM)] + vmem_specs(2 * quarters + 1),
        out_specs=vmem_specs(quarters),
        out_shape=[jax.ShapeDtypeStruct((2 * local * BLOCK, BLOCK), bf16)] * quarters,
        scratch_shapes=[
            band, band, store, whole, pltpu.VMEM((quarters, local, WIDE, BLOCK), bf16),
            pltpu.VMEM((parts, 8, BLOCK), f32),
        ],
        compiler_params=pltpu.CompilerParams(vmem_limit_bytes=20 * 1024 * 1024),
        cost_estimate=pl.CostEstimate(flops=1000, bytes_accessed=1000, transcendentals=0),
        name="sums",
    )(place, *ab_in, *r_in)
    back = [done[0]] + [swap(done[j], j) for j in range(1, quarters)]
    token = lax.ppermute(done[0], "dp", [(i, i ^ 1) for i in range(dp_count)])
    (shares,) = call(
        lambda *refs: lags_kernel(quarters, *refs), "lags", place, ab_in + r_in,
        [jax.ShapeDtypeStruct((owners, BLOCK), f32)], [store, whole, pltpu.VMEM((local, K), f32)],
        flops=1000, nbytes=1000, after=[token],
    )
    arrived = lax.all_to_all(shares, every, 0, 0, tiled=True)

    early, last = [0, quarters - 1], list(range(1, quarters - 1))
    outputs = gate_outputs(early, place, back, gates)
    output, grad_pre, grad_post, grad_values = gate_outputs(last, place, back, gates, outputs)
    total_tokens = dp_count * parts * pre_gate.shape[1] * (channels // groups)
    (mine,) = call(
        lambda *refs: owned_kernel(1.0 / float(total_tokens**0.5), *refs), "owned", place, [arrived],
        [jax.ShapeDtypeStruct((groups, rows), f32)], flops=1000, nbytes=1000,
    )
    return output, grad_pre, grad_post, grad_values, mine.T


def solution(mesh):
    def chosen(*shard):
        fits = swap_fits(*shard)
        return (swapped if fits else shards)(*shard)

    return jax.shard_map(
        chosen,
        mesh=mesh,
        in_specs=(
            P("dp", "seq", None),
            P("dp", "seq", None),
            P("dp", "seq", None),
            P("dp", "seq", None),
            P(("dp", "seq"), None),
        ),
        out_specs=(
            P("dp", "seq", None),
            P("dp", "seq", None),
            P("dp", "seq", None),
            P("dp", "seq", None),
            P(("dp", "seq"), None),
        ),
        check_vma=False,
    )
```

```python
import jax
import jax.numpy as jnp
import numpy as np
from jax import lax
from jax.experimental import pallas as pl
from jax.experimental.pallas import tpu as pltpu
from jax.sharding import PartitionSpec as P

K = 1024


def shifted(value, axis, steps):
    count = lax.axis_size(axis)
    first, last = (max(0, -steps), min(count, count - steps))
    return lax.ppermute(value, axis, [(source, source + steps) for source in range(first, last)])


def tile_index(lag_blocks, shard_len):
    offsets = np.arange(lag_blocks)[:, None, None] * shard_len
    rows_idx = np.arange(shard_len)[None, :, None]
    cols_idx = np.arange(shard_len)[None, None, :]
    return (offsets + rows_idx - cols_idx + shard_len).astype(np.int32)


def build_tiles(all_taps, lag_blocks, shard_len):
    tap_count = all_taps.shape[0]
    needed = (lag_blocks + 1) * shard_len
    trailing = max(needed - shard_len - tap_count, 0)
    padded = jnp.concatenate(
        [
            jnp.zeros((shard_len, all_taps.shape[1]), all_taps.dtype),
            all_taps,
            jnp.zeros((trailing, all_taps.shape[1]), all_taps.dtype),
        ],
        axis=0,
    )
    columns = padded.T
    return columns[:, tile_index(lag_blocks, shard_len)]


def earlier_relay(piece_in, history_len):

    def earlier_advance(moving, unused):
        arrived = shifted(moving, "seq", 1)
        return (arrived, arrived)

    unused_last, stacked = lax.scan(earlier_advance, piece_in, None, length=history_len)
    return jnp.concatenate([piece_in[None], stacked], axis=0)


def later_relay(piece_in, history_len):

    def later_advance(moving, unused):
        arrived = shifted(moving, "seq", -1)
        return (arrived, arrived)

    unused_last, stacked = lax.scan(later_advance, piece_in, None, length=history_len)
    return jnp.concatenate([piece_in[None], stacked], axis=0)


def lag_window(gated_rows, history, local_groups, group_width, lag_count):
    row_count = gated_rows.shape[0]
    span_len = history.shape[0]
    front_zero = jnp.zeros((row_count, history.shape[1]), history.dtype)
    widened = jnp.concatenate([front_zero, history], axis=0)
    gated_grp = gated_rows.reshape(row_count, local_groups, group_width).transpose(1, 0, 2)
    hist_grp = widened.reshape(span_len + row_count, local_groups, group_width).transpose(1, 0, 2)

    def one_group(pair_in):
        gated_one, hist_one = pair_in
        product = lax.dot_general(
            gated_one, hist_one, (((1,), (1,)), ((), ())), preferred_element_type=jnp.float32
        )
        padded = jnp.pad(product, ((0, 0), (0, row_count)))
        flat_line = jnp.concatenate(
            [padded.reshape(-1), jnp.zeros((row_count,), jnp.float32)], axis=0
        )
        skewed = flat_line.reshape(row_count, span_len + 2 * row_count + 1)
        diag_sums = jnp.sum(skewed, axis=0)
        return jnp.flip(diag_sums[1 : span_len + 1], axis=0)[:lag_count]

    return lax.map(one_group, (gated_grp, hist_grp))


def shards(pre_gate, post_gate, values, cotangent, filters):
    shard_len = pre_gate.shape[1]
    channels = pre_gate.shape[2]
    groups = filters.shape[1]
    group_size = channels // groups
    seq_count = lax.axis_size("seq")
    all_taps = lax.all_gather(filters, ("dp", "seq"), axis=0, tiled=True)
    mixed_in = (pre_gate[0].astype(jnp.float32) * values[0]).astype(jnp.bfloat16)
    gated = (cotangent[0].astype(jnp.float32) * post_gate[0]).astype(jnp.bfloat16)
    history_len = min(-(-K // shard_len), seq_count - 1)
    lag_blocks = history_len + 1
    mixed_ext = earlier_relay(mixed_in, history_len)
    gated_ext = later_relay(gated, history_len)
    mixed_four = mixed_ext.reshape(lag_blocks, shard_len, groups, group_size)
    gated_four = gated_ext.reshape(lag_blocks, shard_len, groups, group_size)
    tiles = build_tiles(all_taps, lag_blocks, shard_len)
    convolved = jnp.einsum(
        "gmij,mjgc->igc", tiles, mixed_four, preferred_element_type=jnp.float32
    ).reshape(shard_len, channels)
    carried = jnp.einsum(
        "gmji,mjgc->igc", tiles, gated_four, preferred_element_type=jnp.float32
    ).reshape(shard_len, channels)
    hist_len = lag_blocks * shard_len
    lag_count = min(K, hist_len)
    history = jnp.flip(mixed_ext, axis=0).reshape(hist_len, channels)
    lag_local = lag_window(gated, history, groups, group_size, lag_count)
    partial_grads = lag_local.T
    output = (post_gate[0].astype(jnp.float32) * convolved).astype(jnp.bfloat16)
    grad_post = (cotangent[0].astype(jnp.float32) * convolved).astype(jnp.bfloat16)
    grad_pre = (carried * values[0]).astype(jnp.bfloat16)
    grad_values = (carried * pre_gate[0]).astype(jnp.bfloat16)
    owned = lax.psum_scatter(partial_grads, ("dp", "seq"), scatter_dimension=0, tiled=True)
    total_tokens = lax.axis_size("dp") * shard_len * seq_count * group_size
    grad_filters = owned / float(total_tokens**0.5)
    return (output[None], grad_pre[None], grad_post[None], grad_values[None], grad_filters)


BLOCK = 128


def swap_fits(pre_gate, post_gate, values, cotangent, filters):
    parts, dp_count = lax.axis_size("seq"), lax.axis_size("dp")
    channels, groups = pre_gate.shape[2], filters.shape[1]
    return (
        parts >= 4
        and parts & (parts - 1) == 0
        and groups % parts == 0
        and channels // groups == BLOCK
        and pre_gate.shape[0] == 1
        and pre_gate.shape[1] == BLOCK
        and parts * BLOCK == K
        and filters.shape[0] * parts * dp_count == K
        and dp_count == parts // 2 == groups // (parts // 2)
    )


def swap(chunk, flip):
    count = lax.axis_size("seq")
    return lax.ppermute(chunk, "seq", [(i, i ^ flip) for i in range(count)])


def vmem_specs(count):
    return [pl.BlockSpec(memory_space=pltpu.VMEM)] * count


def chunk_shapes(count, width, blocks=1):
    return [jax.ShapeDtypeStruct((blocks * BLOCK, width), jnp.bfloat16)] * count


def call(kernel, name, place, operands, out_shape, scratch=(), flops=1000, nbytes=1000, after=()):
    def body(place_ref, *refs):
        kernel(place_ref, *refs[: len(operands)], *refs[len(operands) + len(after) :])

    return pl.pallas_call(
        body,
        in_specs=[pl.BlockSpec(memory_space=pltpu.SMEM)]
        + vmem_specs(len(operands))
        + [pl.BlockSpec(memory_space=pl.ANY)] * len(after),
        out_specs=vmem_specs(len(out_shape)),
        out_shape=out_shape,
        scratch_shapes=list(scratch),
        compiler_params=pltpu.CompilerParams(vmem_limit_bytes=20 * 1024 * 1024),
        cost_estimate=pl.CostEstimate(flops=flops, bytes_accessed=nbytes, transcendentals=0),
        name=name,
    )(place, *operands, *after)


TAIL = 16
SPLIT = 2


def pack_kernel(quarters, pieces, place_ref, *refs):
    f32, bf16 = jnp.float32, jnp.bfloat16
    taps_in, (a_ref, b_ref), refs = refs[:pieces], refs[pieces : pieces + 2], refs[pieces + 2 :]
    a_outs, outs, (taps_ref,) = refs[:quarters], refs[quarters : 2 * quarters], refs[2 * quarters :]
    quarter = place_ref[1]
    local = taps_ref.shape[1]
    taps = jnp.concatenate([piece[...].astype(f32) for piece in taps_in], axis=1)
    for i in range(quarters):
        taps_ref[i] = taps[i * local : (i + 1) * local]
    for j in range(quarters):
        for g in range(local):
            columns = pl.ds(pl.multiple_of(((quarter ^ j) * local + g) * BLOCK, BLOCK), BLOCK)
            a = a_ref[:, columns]
            a_outs[j][g * BLOCK : (g + 1) * BLOCK] = a
            if j != SPLIT:
                outs[j][g * BLOCK : (g + 1) * BLOCK] = a
                outs[j][(local + g) * BLOCK : (local + g + 1) * BLOCK] = b_ref[:, columns]
            else:
                outs[j][g * BLOCK : (g + 1) * BLOCK] = b_ref[:, columns]
        tail = jnp.concatenate([taps_ref[quarter ^ j], jnp.zeros((TAIL - local, BLOCK), f32)], axis=0).astype(bf16)
        a_outs[j][local * BLOCK :] = tail
        outs[j][-TAIL:] = tail


def bands(quarters, dp_count, place_ref, taps_in, taps_ref, causal_ref, anti_ref, causal_from, anti_to):
    half, quarter, dp_index = place_ref[0], place_ref[1], place_ref[2]
    for u in range(2):
        for j in range(quarters):
            tail = taps_in[u * quarters + j][-TAIL:].astype(jnp.float32)
            taps_ref[(half ^ u) * quarters + (quarter ^ j)] = tail[: taps_ref.shape[1]]
    rows = BLOCK // dp_count
    part = lax.broadcasted_iota(jnp.int32, (1, BLOCK), 1) // rows
    blocks = []
    for d in range(dp_count):
        way = dp_index ^ d
        for h in range(2):
            block = None
            for q in range(quarters):
                shift = lax.rem(q + dp_count - way, dp_count) * rows
                moved = pltpu.roll(taps_ref[h * quarters + q], shift, 1)
                block = moved if block is None else jnp.where(part == q, moved, block)
            blocks.append(block)
    for g in range(causal_ref.shape[0]):
        line = jnp.concatenate([block[g : g + 1] for block in blocks] + [jnp.zeros((1, BLOCK), jnp.float32)], axis=1)
        shear = pltpu.roll(jnp.broadcast_to(line, (BLOCK, K + BLOCK)), 0, 1, stride=1, stride_axis=0)
        zero = jnp.zeros((BLOCK, BLOCK), jnp.bfloat16)
        count = K // BLOCK
        tiles = [shear[:, m * BLOCK : (m + 1) * BLOCK] for m in range(count)]
        for b in range(anti_to // BLOCK):
            columns = slice(b * BLOCK, (b + 1) * BLOCK)
            anti_ref[g, :BLOCK, columns] = tiles[b].astype(jnp.bfloat16)
            anti_ref[g, BLOCK:, columns] = tiles[b - 1].astype(jnp.bfloat16) if b else zero
        wanted = count - causal_from // BLOCK
        turned = [tile.T.astype(jnp.bfloat16) for tile in tiles[:wanted]] + [zero]
        for b in range(count - wanted, count):
            columns = slice(b * BLOCK, (b + 1) * BLOCK)
            causal_ref[g, :BLOCK, columns] = turned[count - 2 - b] if b < count - 1 else zero
            causal_ref[g, BLOCK:, columns] = turned[count - 1 - b]


def rows_of(ref, lanes):
    return ref[:, :, lanes].reshape(ref.shape[0] * BLOCK, BLOCK)


def dot(left, right):
    return jnp.dot(left, right, preferred_element_type=jnp.float32)


WIDE = 2 * BLOCK


def side_by_side(data):
    return jnp.concatenate([data[:-WIDE], data[WIDE:]], axis=1)


def causal_part(band, data):
    length = data.shape[0]
    both = dot(band[:, K - length + WIDE :], side_by_side(data))
    return both[:, :BLOCK], both[:, BLOCK:] + dot(band[:, K - length : K - length + WIDE], data[:WIDE])


def anti_part(band, data):
    length = data.shape[0]
    both = dot(band[:, : length - WIDE], side_by_side(data))
    return both[:, :BLOCK] + dot(band[:, length - WIDE : length], data[-WIDE:]), both[:, BLOCK:]


def lag_lines(mixed, mixed_first, gated, gated_first):
    count = mixed.shape[0] // BLOCK
    blocks = K // BLOCK
    still = [mixed[j * BLOCK : (j + 1) * BLOCK] for j in range(count)]
    ready = [gated[i * BLOCK : (i + 1) * BLOCK] for i in range(gated.shape[0] // BLOCK)]
    sums = [None] * blocks
    for lag in range(blocks):
        pairs = [(j, j + lag + mixed_first - gated_first) for j in range(count)]
        pairs = [(j, i) for j, i in pairs if 0 <= i < len(ready)]
        if pairs:
            left = jnp.concatenate([still[j] for j, _ in pairs], axis=1)
            right = jnp.concatenate([ready[i] for _, i in pairs], axis=1)
            sums[lag] = lax.dot_general(left, right, (((1,), (1,)), ((), ())), preferred_element_type=jnp.float32)
    last = max(m for m in range(blocks) if sums[m] is not None)
    zero = jnp.zeros((BLOCK, BLOCK), jnp.float32)
    table = jnp.concatenate([zero if term is None else term for term in sums[: last + 1]] + [zero], axis=1)
    span = (last + 2) * BLOCK
    parts, step = [table[row : row + 8] for row in range(0, BLOCK, 8)], 8
    while len(parts) > 1:
        parts = [near + pltpu.roll(far, span - step, 1) for near, far in zip(parts[::2], parts[1::2])]
        step *= 2
    total = parts[0]
    row = lax.broadcasted_iota(jnp.int32, (8, span), 0)
    for step in (1, 2, 4):
        total = jnp.where((row & step) != 0, pltpu.roll(total, span - step, 1), total)
    line = jnp.sum(total, axis=0, keepdims=True)[:, : span - BLOCK]
    if span - BLOCK < K:
        line = jnp.concatenate([line, jnp.zeros((1, K + BLOCK - span), jnp.float32)], axis=1)
    return line


def gather(quarters, place_ref, ab_in, r_in, a_ref, data_ref):
    half, quarter = place_ref[0], place_ref[1]
    local = a_ref.shape[2] // BLOCK
    for j in range(quarters):
        b_in, b_row = (ab_in[j], local) if j != SPLIT else (ab_in[quarters], 0)
        for g in range(local):
            lanes = slice(g * BLOCK, (g + 1) * BLOCK)
            a_ref[quarter ^ j, :, lanes] = ab_in[j][g * BLOCK : (g + 1) * BLOCK]
            b_rows = slice((b_row + g) * BLOCK, (b_row + g + 1) * BLOCK)
            data_ref[half * quarters + (quarter ^ j), :, lanes] = b_in[b_rows]
            data_ref[(1 - half) * quarters + (quarter ^ j), :, lanes] = r_in[j][g * BLOCK : (g + 1) * BLOCK]


def lags_kernel(quarters, place_ref, *refs):
    ab_in, r_in, refs = refs[: quarters + 1], refs[quarters + 1 : 2 * quarters + 1], refs[2 * quarters + 1 :]
    shares_ref, a_ref, data_ref, lines_ref = refs
    gather(quarters, place_ref, ab_in, r_in, a_ref, data_ref)
    half = place_ref[0]
    local = lines_ref.shape[0]
    length = quarters * BLOCK

    @pl.when(half == 0)
    def lower():
        for g in range(local):
            lanes = slice(g * BLOCK, (g + 1) * BLOCK)
            mixed, gated = rows_of(a_ref, lanes), rows_of(data_ref, lanes)
            lines_ref[g : g + 1] = lag_lines(mixed, 0, gated if g < local // 2 else gated[:length], 0)

    @pl.when(half != 0)
    def upper():
        for g in range(local):
            lanes = slice(g * BLOCK, (g + 1) * BLOCK)
            gated, mixed = rows_of(a_ref, lanes), rows_of(data_ref, lanes)
            first = quarters if g < local // 2 else 0
            lines_ref[g : g + 1] = lag_lines(mixed[first * BLOCK :], first, gated, quarters)

    step = BLOCK // local
    owners = shares_ref.shape[0]
    for block in range(K // BLOCK):
        shares_ref[block * local : (block + 1) * local] = lines_ref[:, block * BLOCK : (block + 1) * BLOCK]
    rows = shares_ref[...]
    way = lax.broadcasted_iota(jnp.int32, rows.shape, 1) // step - lax.broadcasted_iota(jnp.int32, rows.shape, 0) % local
    sorted_rows = rows
    for d in range(1 - local, local):
        if d:
            moved = pltpu.roll(pltpu.roll(rows, -d % owners, 0), d * step % BLOCK, 1)
            sorted_rows = jnp.where(way == d, moved, sorted_rows)
    shares_ref[...] = sorted_rows


def sums_kernel(quarters, dp_count, place_ref, *refs):
    ab_in, r_in, refs = refs[: quarters + 1], refs[quarters + 1 : 2 * quarters + 1], refs[2 * quarters + 1 :]
    outs, refs = refs[:quarters], refs[quarters:]
    causal_ref, anti_ref, a_ref, data_ref, done_ref, taps_ref = refs
    gather(quarters, place_ref, ab_in, r_in, a_ref, data_ref)
    tails = ab_in[:quarters] + r_in
    half, quarter = place_ref[0], place_ref[1]
    local = causal_ref.shape[0]

    def work(a_part, a_band, b_part, b_band):
        for g in range(local):
            lanes = slice(g * BLOCK, (g + 1) * BLOCK)
            for rows, sums in (
                (slice(0, BLOCK), a_part(a_band.at[g], rows_of(a_ref, lanes))),
                (slice(BLOCK, WIDE), b_part(b_band.at[g], rows_of(data_ref, lanes))),
            ):
                for p in range(2):
                    done_ref[2 * p : 2 * p + 2, g, rows] = sums[p].reshape(2, BLOCK, BLOCK).astype(jnp.bfloat16)

    @pl.when(half == 0)
    def lower():
        bands(quarters, dp_count, place_ref, tails, taps_ref, causal_ref, anti_ref, K // 2, K)
        work(causal_part, causal_ref, anti_part, anti_ref)

    @pl.when(half != 0)
    def upper():
        bands(quarters, dp_count, place_ref, tails, taps_ref, causal_ref, anti_ref, 0, K // 2)
        work(anti_part, anti_ref, causal_part, causal_ref)

    for j in range(quarters):
        outs[j][...] = done_ref[quarter ^ j].reshape(local * WIDE, BLOCK)


def owned_kernel(scale, place_ref, arrived_ref, out_ref):
    groups, rows = out_ref.shape
    local = BLOCK // rows
    quarters = groups // local
    total = arrived_ref[:quarters]
    for i in range(1, arrived_ref.shape[0] // quarters):
        total = total + arrived_ref[i * quarters : (i + 1) * quarters]
    total = total * scale
    for g in range(local):
        part = (total if g == 0 else pltpu.roll(total, BLOCK - g * rows, 1))[:, :rows]
        for q in range(quarters):
            out_ref[q * local + g : q * local + g + 1] = part[q : q + 1]


def outputs_kernel(js, place_ref, *refs):
    f32, bf16 = jnp.float32, jnp.bfloat16
    count = len(js)
    back, inputs = refs[:count], refs[count : count + 4]
    outputs, results, sem = refs[-9:-5], refs[-5:-1], refs[-1]
    half, quarter = place_ref[0], place_ref[1]
    width = results[0].shape[2]

    def copies(i):
        columns = pl.ds(pl.multiple_of((quarter ^ js[i]) * width, width), width)
        return [
            pltpu.make_async_copy(store.at[i], target.at[0, :, columns], sem.at[i, k])
            for k, (store, target) in enumerate(zip(results, outputs))
        ]

    for i in range(count):
        for g in range(width // BLOCK):
            lanes = slice(g * BLOCK, (g + 1) * BLOCK)
            columns = pl.ds(pl.multiple_of((quarter ^ js[i]) * width + g * BLOCK, BLOCK), BLOCK)
            pre, post, values, cot = [source[0, :, columns].astype(f32) for source in inputs]
            sums = back[i][g * WIDE : (g + 1) * WIDE].astype(f32)
            a_sum, b_sum = sums[:BLOCK], sums[BLOCK:]
            convolved, carried = jnp.where(half == 0, a_sum, b_sum), jnp.where(half == 0, b_sum, a_sum)
            for result, value in zip(results, (post * convolved, carried * values, cot * convolved, carried * pre)):
                result[i, :, lanes] = value.astype(bf16)
        for copy in copies(i):
            copy.start()
    for i in range(count):
        for copy in copies(i):
            copy.wait()


def gate_outputs(js, place, back, gates, earlier=()):
    hbm = [pl.BlockSpec(memory_space=pltpu.HBM)] * 4
    store = pltpu.VMEM((len(js), BLOCK, back[0].shape[0] // 2), jnp.bfloat16)
    return pl.pallas_call(
        lambda *refs: outputs_kernel(js, *refs),
        in_specs=[pl.BlockSpec(memory_space=pltpu.SMEM)] + vmem_specs(len(js) + 4) + hbm[: len(earlier)],
        out_specs=hbm,
        out_shape=[jax.ShapeDtypeStruct(gates[0].shape, jnp.bfloat16)] * 4,
        input_output_aliases={1 + len(js) + 4 + k: k for k in range(len(earlier))},
        scratch_shapes=[store] * 4 + [pltpu.SemaphoreType.DMA((len(js), 4))],
        compiler_params=pltpu.CompilerParams(vmem_limit_bytes=20 * 1024 * 1024),
        cost_estimate=pl.CostEstimate(flops=1000, bytes_accessed=1000, transcendentals=0),
        name="outputs",
    )(place, *[back[j] for j in js], *gates, *earlier)


def swapped(pre_gate, post_gate, values, cotangent, filters):
    parts, dp_count = lax.axis_size("seq"), lax.axis_size("dp")
    quarters = parts // 2
    channels, groups = pre_gate.shape[2], filters.shape[1]
    width, local = channels // quarters, groups // quarters
    seq_index = lax.axis_index("seq")
    place = jnp.stack([seq_index // quarters, seq_index % quarters, lax.axis_index("dp")]).astype(jnp.int32)
    owners = parts * dp_count
    rows = filters.shape[0]
    f32, bf16 = jnp.float32, jnp.bfloat16
    every = ("dp", "seq")

    taps = filters.T
    pieces = [taps]
    for p in range(1, dp_count):
        pieces.append(lax.ppermute(taps, "dp", [(i, i ^ p) for i in range(dp_count)]))

    gates = [pre_gate, post_gate, values, cotangent]
    lower = seq_index < quarters
    mixed = (pre_gate[0].astype(f32) * values[0]).astype(bf16)
    gated = (cotangent[0].astype(f32) * post_gate[0]).astype(bf16)
    a, b = jnp.where(lower, mixed, gated), jnp.where(lower, gated, mixed)
    store = pltpu.VMEM((quarters, BLOCK, width), bf16)
    short = jax.ShapeDtypeStruct((local * BLOCK + TAIL, BLOCK), bf16)
    message = jax.ShapeDtypeStruct((2 * local * BLOCK + TAIL, BLOCK), bf16)
    chunks = call(
        lambda *refs: pack_kernel(quarters, dp_count, *refs), "pack", place, pieces + [a, b],
        [short] * quarters + [short if j == SPLIT else message for j in range(quarters)], [pltpu.VMEM((quarters, local, BLOCK), f32)],
        flops=1000, nbytes=1000,
    )
    a_own, ab_own = chunks[:quarters], chunks[quarters:]
    r_in = [swap(a_own[j], quarters + j) for j in range(quarters)]
    ab_in = [ab_own[0]] + [swap(a_own[j] if j == SPLIT else ab_own[j], j) for j in range(1, quarters)]
    ab_in.append(swap(ab_own[SPLIT], SPLIT))

    band = pltpu.VMEM((local, 2 * BLOCK, K), bf16)
    store = pltpu.VMEM((quarters, BLOCK, width), bf16)
    whole = pltpu.VMEM((parts, BLOCK, width), bf16)
    done = pl.pallas_call(
        lambda *refs: sums_kernel(quarters, dp_count, *refs),
        in_specs=[pl.BlockSpec(memory_space=pltpu.SMEM)] + vmem_specs(2 * quarters + 1),
        out_specs=vmem_specs(quarters),
        out_shape=[jax.ShapeDtypeStruct((2 * local * BLOCK, BLOCK), bf16)] * quarters,
        scratch_shapes=[
            band, band, store, whole, pltpu.VMEM((quarters, local, WIDE, BLOCK), bf16),
            pltpu.VMEM((parts, 8, BLOCK), f32),
        ],
        compiler_params=pltpu.CompilerParams(vmem_limit_bytes=20 * 1024 * 1024),
        cost_estimate=pl.CostEstimate(flops=1000, bytes_accessed=1000, transcendentals=0),
        name="sums",
    )(place, *ab_in, *r_in)
    back = [done[0]] + [swap(done[j], j) for j in range(1, quarters)]
    token = lax.ppermute(done[0], "dp", [(i, i ^ 1) for i in range(dp_count)])
    (shares,) = call(
        lambda *refs: lags_kernel(quarters, *refs), "lags", place, ab_in + r_in,
        [jax.ShapeDtypeStruct((owners, BLOCK), f32)], [store, whole, pltpu.VMEM((local, K), f32)],
        flops=1000, nbytes=1000, after=[token],
    )
    arrived = lax.all_to_all(shares, every, 0, 0, tiled=True)

    early, last = [0, quarters - 1], list(range(1, quarters - 1))
    outputs = gate_outputs(early, place, back, gates)
    output, grad_pre, grad_post, grad_values = gate_outputs(last, place, back, gates, outputs)
    total_tokens = dp_count * parts * pre_gate.shape[1] * (channels // groups)
    (mine,) = call(
        lambda *refs: owned_kernel(1.0 / float(total_tokens**0.5), *refs), "owned", place, [arrived],
        [jax.ShapeDtypeStruct((groups, rows), f32)], flops=1000, nbytes=1000,
    )
    return output, grad_pre, grad_post, grad_values, mine.T


def solution(mesh):
    def chosen(*shard):
        fits = swap_fits(*shard)
        return (swapped if fits else shards)(*shard)

    return jax.shard_map(
        chosen,
        mesh=mesh,
        in_specs=(
            P("dp", "seq", None),
            P("dp", "seq", None),
            P("dp", "seq", None),
            P("dp", "seq", None),
            P(("dp", "seq"), None),
        ),
        out_specs=(
            P("dp", "seq", None),
            P("dp", "seq", None),
            P("dp", "seq", None),
            P("dp", "seq", None),
            P(("dp", "seq"), None),
        ),
        check_vma=False,
    )
```

```python
import jax
import jax.numpy as jnp
import numpy as np
from jax import lax
from jax.experimental import pallas as pl
from jax.experimental.pallas import tpu as pltpu
from jax.sharding import PartitionSpec as P

K = 1024


def shifted(value, axis, steps):
    count = lax.axis_size(axis)
    first, last = (max(0, -steps), min(count, count - steps))
    return lax.ppermute(value, axis, [(source, source + steps) for source in range(first, last)])


def tile_index(lag_blocks, shard_len):
    offsets = np.arange(lag_blocks)[:, None, None] * shard_len
    rows_idx = np.arange(shard_len)[None, :, None]
    cols_idx = np.arange(shard_len)[None, None, :]
    return (offsets + rows_idx - cols_idx + shard_len).astype(np.int32)


def build_tiles(all_taps, lag_blocks, shard_len):
    tap_count = all_taps.shape[0]
    needed = (lag_blocks + 1) * shard_len
    trailing = max(needed - shard_len - tap_count, 0)
    padded = jnp.concatenate(
        [
            jnp.zeros((shard_len, all_taps.shape[1]), all_taps.dtype),
            all_taps,
            jnp.zeros((trailing, all_taps.shape[1]), all_taps.dtype),
        ],
        axis=0,
    )
    columns = padded.T
    return columns[:, tile_index(lag_blocks, shard_len)]


def earlier_relay(piece_in, history_len):

    def earlier_advance(moving, unused):
        arrived = shifted(moving, "seq", 1)
        return (arrived, arrived)

    unused_last, stacked = lax.scan(earlier_advance, piece_in, None, length=history_len)
    return jnp.concatenate([piece_in[None], stacked], axis=0)


def later_relay(piece_in, history_len):

    def later_advance(moving, unused):
        arrived = shifted(moving, "seq", -1)
        return (arrived, arrived)

    unused_last, stacked = lax.scan(later_advance, piece_in, None, length=history_len)
    return jnp.concatenate([piece_in[None], stacked], axis=0)


def lag_window(gated_rows, history, local_groups, group_width, lag_count):
    row_count = gated_rows.shape[0]
    span_len = history.shape[0]
    front_zero = jnp.zeros((row_count, history.shape[1]), history.dtype)
    widened = jnp.concatenate([front_zero, history], axis=0)
    gated_grp = gated_rows.reshape(row_count, local_groups, group_width).transpose(1, 0, 2)
    hist_grp = widened.reshape(span_len + row_count, local_groups, group_width).transpose(1, 0, 2)

    def one_group(pair_in):
        gated_one, hist_one = pair_in
        product = lax.dot_general(
            gated_one, hist_one, (((1,), (1,)), ((), ())), preferred_element_type=jnp.float32
        )
        padded = jnp.pad(product, ((0, 0), (0, row_count)))
        flat_line = jnp.concatenate(
            [padded.reshape(-1), jnp.zeros((row_count,), jnp.float32)], axis=0
        )
        skewed = flat_line.reshape(row_count, span_len + 2 * row_count + 1)
        diag_sums = jnp.sum(skewed, axis=0)
        return jnp.flip(diag_sums[1 : span_len + 1], axis=0)[:lag_count]

    return lax.map(one_group, (gated_grp, hist_grp))


def shards(pre_gate, post_gate, values, cotangent, filters):
    shard_len = pre_gate.shape[1]
    channels = pre_gate.shape[2]
    groups = filters.shape[1]
    group_size = channels // groups
    seq_count = lax.axis_size("seq")
    all_taps = lax.all_gather(filters, ("dp", "seq"), axis=0, tiled=True)
    mixed_in = (pre_gate[0].astype(jnp.float32) * values[0]).astype(jnp.bfloat16)
    gated = (cotangent[0].astype(jnp.float32) * post_gate[0]).astype(jnp.bfloat16)
    history_len = min(-(-K // shard_len), seq_count - 1)
    lag_blocks = history_len + 1
    mixed_ext = earlier_relay(mixed_in, history_len)
    gated_ext = later_relay(gated, history_len)
    mixed_four = mixed_ext.reshape(lag_blocks, shard_len, groups, group_size)
    gated_four = gated_ext.reshape(lag_blocks, shard_len, groups, group_size)
    tiles = build_tiles(all_taps, lag_blocks, shard_len)
    convolved = jnp.einsum(
        "gmij,mjgc->igc", tiles, mixed_four, preferred_element_type=jnp.float32
    ).reshape(shard_len, channels)
    carried = jnp.einsum(
        "gmji,mjgc->igc", tiles, gated_four, preferred_element_type=jnp.float32
    ).reshape(shard_len, channels)
    hist_len = lag_blocks * shard_len
    lag_count = min(K, hist_len)
    history = jnp.flip(mixed_ext, axis=0).reshape(hist_len, channels)
    lag_local = lag_window(gated, history, groups, group_size, lag_count)
    partial_grads = lag_local.T
    output = (post_gate[0].astype(jnp.float32) * convolved).astype(jnp.bfloat16)
    grad_post = (cotangent[0].astype(jnp.float32) * convolved).astype(jnp.bfloat16)
    grad_pre = (carried * values[0]).astype(jnp.bfloat16)
    grad_values = (carried * pre_gate[0]).astype(jnp.bfloat16)
    owned = lax.psum_scatter(partial_grads, ("dp", "seq"), scatter_dimension=0, tiled=True)
    total_tokens = lax.axis_size("dp") * shard_len * seq_count * group_size
    grad_filters = owned / float(total_tokens**0.5)
    return (output[None], grad_pre[None], grad_post[None], grad_values[None], grad_filters)


BLOCK = 128


def swap_fits(pre_gate, post_gate, values, cotangent, filters):
    parts, dp_count = lax.axis_size("seq"), lax.axis_size("dp")
    channels, groups = pre_gate.shape[2], filters.shape[1]
    return (
        parts >= 4
        and parts & (parts - 1) == 0
        and groups % parts == 0
        and channels // groups == BLOCK
        and pre_gate.shape[0] == 1
        and pre_gate.shape[1] == BLOCK
        and parts * BLOCK == K
        and filters.shape[0] * parts * dp_count == K
        and dp_count == parts // 2 == groups // (parts // 2)
    )


def swap(chunk, flip):
    count = lax.axis_size("seq")
    return lax.ppermute(chunk, "seq", [(i, i ^ flip) for i in range(count)])


def vmem_specs(count):
    return [pl.BlockSpec(memory_space=pltpu.VMEM)] * count


def chunk_shapes(count, width, blocks=1):
    return [jax.ShapeDtypeStruct((blocks * BLOCK, width), jnp.bfloat16)] * count


def call(kernel, name, place, operands, out_shape, scratch=(), flops=1000, nbytes=1000, after=()):
    def body(place_ref, *refs):
        kernel(place_ref, *refs[: len(operands)], *refs[len(operands) + len(after) :])

    return pl.pallas_call(
        body,
        in_specs=[pl.BlockSpec(memory_space=pltpu.SMEM)]
        + vmem_specs(len(operands))
        + [pl.BlockSpec(memory_space=pl.ANY)] * len(after),
        out_specs=vmem_specs(len(out_shape)),
        out_shape=out_shape,
        scratch_shapes=list(scratch),
        compiler_params=pltpu.CompilerParams(vmem_limit_bytes=20 * 1024 * 1024),
        cost_estimate=pl.CostEstimate(flops=flops, bytes_accessed=nbytes, transcendentals=0),
        name=name,
    )(place, *operands, *after)


TAIL = 16
SPLIT = 2


def pack_kernel(quarters, pieces, place_ref, *refs):
    f32, bf16 = jnp.float32, jnp.bfloat16
    taps_in, (a_ref, b_ref), refs = refs[:pieces], refs[pieces : pieces + 2], refs[pieces + 2 :]
    a_outs, outs, (taps_ref,) = refs[:quarters], refs[quarters : 2 * quarters], refs[2 * quarters :]
    quarter = place_ref[1]
    local = taps_ref.shape[1]
    taps = jnp.concatenate([piece[...].astype(f32) for piece in taps_in], axis=1)
    for i in range(quarters):
        taps_ref[i] = taps[i * local : (i + 1) * local]
    for j in range(quarters):
        for g in range(local):
            columns = pl.ds(pl.multiple_of(((quarter ^ j) * local + g) * BLOCK, BLOCK), BLOCK)
            a = a_ref[:, columns]
            a_outs[j][g * BLOCK : (g + 1) * BLOCK] = a
            if j != SPLIT:
                outs[j][g * BLOCK : (g + 1) * BLOCK] = a
                outs[j][(local + g) * BLOCK : (local + g + 1) * BLOCK] = b_ref[:, columns]
            else:
                outs[j][g * BLOCK : (g + 1) * BLOCK] = b_ref[:, columns]
        tail = jnp.concatenate([taps_ref[quarter ^ j], jnp.zeros((TAIL - local, BLOCK), f32)], axis=0).astype(bf16)
        a_outs[j][local * BLOCK :] = tail
        outs[j][-TAIL:] = tail


def bands(quarters, dp_count, place_ref, taps_in, taps_ref, causal_ref, anti_ref, causal_from, anti_to):
    half, quarter, dp_index = place_ref[0], place_ref[1], place_ref[2]
    for u in range(2):
        for j in range(quarters):
            tail = taps_in[u * quarters + j][-TAIL:].astype(jnp.float32)
            taps_ref[(half ^ u) * quarters + (quarter ^ j)] = tail[: taps_ref.shape[1]]
    rows = BLOCK // dp_count
    part = lax.broadcasted_iota(jnp.int32, (1, BLOCK), 1) // rows
    blocks = []
    for d in range(dp_count):
        way = dp_index ^ d
        for h in range(2):
            block = None
            for q in range(quarters):
                shift = lax.rem(q + dp_count - way, dp_count) * rows
                moved = pltpu.roll(taps_ref[h * quarters + q], shift, 1)
                block = moved if block is None else jnp.where(part == q, moved, block)
            blocks.append(block)
    for g in range(causal_ref.shape[0]):
        line = jnp.concatenate([block[g : g + 1] for block in blocks] + [jnp.zeros((1, BLOCK), jnp.float32)], axis=1)
        shear = pltpu.roll(jnp.broadcast_to(line, (BLOCK, K + BLOCK)), 0, 1, stride=1, stride_axis=0)
        zero = jnp.zeros((BLOCK, BLOCK), jnp.bfloat16)
        count = K // BLOCK
        tiles = [shear[:, m * BLOCK : (m + 1) * BLOCK] for m in range(count)]
        for b in range(anti_to // BLOCK):
            columns = slice(b * BLOCK, (b + 1) * BLOCK)
            anti_ref[g, :BLOCK, columns] = tiles[b].astype(jnp.bfloat16)
            anti_ref[g, BLOCK:, columns] = tiles[b - 1].astype(jnp.bfloat16) if b else zero
        wanted = count - causal_from // BLOCK
        turned = [tile.T.astype(jnp.bfloat16) for tile in tiles[:wanted]] + [zero]
        for b in range(count - wanted, count):
            columns = slice(b * BLOCK, (b + 1) * BLOCK)
            causal_ref[g, :BLOCK, columns] = turned[count - 2 - b] if b < count - 1 else zero
            causal_ref[g, BLOCK:, columns] = turned[count - 1 - b]


def rows_of(ref, lanes):
    return ref[:, :, lanes].reshape(ref.shape[0] * BLOCK, BLOCK)


def dot(left, right):
    return jnp.dot(left, right, preferred_element_type=jnp.float32)


WIDE = 2 * BLOCK


def side_by_side(data):
    return jnp.concatenate([data[:-WIDE], data[WIDE:]], axis=1)


def causal_part(band, data):
    length = data.shape[0]
    both = dot(band[:, K - length + WIDE :], side_by_side(data))
    return both[:, :BLOCK], both[:, BLOCK:] + dot(band[:, K - length : K - length + WIDE], data[:WIDE])


def anti_part(band, data):
    length = data.shape[0]
    both = dot(band[:, : length - WIDE], side_by_side(data))
    return both[:, :BLOCK] + dot(band[:, length - WIDE : length], data[-WIDE:]), both[:, BLOCK:]


def lag_lines(mixed, mixed_first, gated, gated_first):
    count = mixed.shape[0] // BLOCK
    blocks = K // BLOCK
    still = [mixed[j * BLOCK : (j + 1) * BLOCK] for j in range(count)]
    ready = [gated[i * BLOCK : (i + 1) * BLOCK] for i in range(gated.shape[0] // BLOCK)]
    sums = [None] * blocks
    for lag in range(blocks):
        pairs = [(j, j + lag + mixed_first - gated_first) for j in range(count)]
        pairs = [(j, i) for j, i in pairs if 0 <= i < len(ready)]
        if pairs:
            left = jnp.concatenate([still[j] for j, _ in pairs], axis=1)
            right = jnp.concatenate([ready[i] for _, i in pairs], axis=1)
            sums[lag] = lax.dot_general(left, right, (((1,), (1,)), ((), ())), preferred_element_type=jnp.float32)
    last = max(m for m in range(blocks) if sums[m] is not None)
    zero = jnp.zeros((BLOCK, BLOCK), jnp.float32)
    table = jnp.concatenate([zero if term is None else term for term in sums[: last + 1]] + [zero], axis=1)
    span = (last + 2) * BLOCK
    parts, step = [table[row : row + 8] for row in range(0, BLOCK, 8)], 8
    while len(parts) > 1:
        parts = [near + pltpu.roll(far, span - step, 1) for near, far in zip(parts[::2], parts[1::2])]
        step *= 2
    total = parts[0]
    row = lax.broadcasted_iota(jnp.int32, (8, span), 0)
    for step in (1, 2, 4):
        total = jnp.where((row & step) != 0, pltpu.roll(total, span - step, 1), total)
    line = jnp.sum(total, axis=0, keepdims=True)[:, : span - BLOCK]
    if span - BLOCK < K:
        line = jnp.concatenate([line, jnp.zeros((1, K + BLOCK - span), jnp.float32)], axis=1)
    return line


def gather(quarters, place_ref, ab_in, r_in, a_ref, data_ref, far=None):
    half, quarter = place_ref[0], place_ref[1]
    local = a_ref.shape[2] // BLOCK
    for j in range(quarters):
        b_in, b_row = (ab_in[j], local) if j != SPLIT else (ab_in[quarters], 0)
        for g in range(local):
            lanes = slice(g * BLOCK, (g + 1) * BLOCK)
            a_ref[quarter ^ j, :, lanes] = ab_in[j][g * BLOCK : (g + 1) * BLOCK]
            b_rows = slice((b_row + g) * BLOCK, (b_row + g + 1) * BLOCK)
            data_ref[half * quarters + (quarter ^ j), :, lanes] = b_in[b_rows]
            if far is None:
                data_ref[(1 - half) * quarters + (quarter ^ j), :, lanes] = r_in[j][g * BLOCK : (g + 1) * BLOCK]


def lags_kernel(quarters, place_ref, *refs):
    ab_in, r_in, refs = refs[: quarters + 1], refs[quarters + 1 : 2 * quarters + 1], refs[2 * quarters + 1 :]
    shares_ref, a_ref, data_ref, lines_ref = refs
    gather(quarters, place_ref, ab_in, r_in, a_ref, data_ref, ())
    half, quarter = place_ref[0], place_ref[1]

    def fetch(first, groups):
        for j in range(quarters):
            for g in groups:
                lanes = slice(g * BLOCK, (g + 1) * BLOCK)
                data_ref[first + (quarter ^ j), :, lanes] = r_in[j][g * BLOCK : (g + 1) * BLOCK]

    local = lines_ref.shape[0]
    length = quarters * BLOCK

    @pl.when(half == 0)
    def lower():
        fetch(quarters, range(local // 2))
        for g in range(local):
            lanes = slice(g * BLOCK, (g + 1) * BLOCK)
            mixed, gated = rows_of(a_ref, lanes), rows_of(data_ref, lanes)
            lines_ref[g : g + 1] = lag_lines(mixed, 0, gated if g < local // 2 else gated[:length], 0)

    @pl.when(half != 0)
    def upper():
        fetch(0, range(local // 2, local))
        for g in range(local):
            lanes = slice(g * BLOCK, (g + 1) * BLOCK)
            gated, mixed = rows_of(a_ref, lanes), rows_of(data_ref, lanes)
            first = quarters if g < local // 2 else 0
            lines_ref[g : g + 1] = lag_lines(mixed[first * BLOCK :], first, gated, quarters)

    step = BLOCK // local
    owners = shares_ref.shape[0]
    for block in range(K // BLOCK):
        shares_ref[block * local : (block + 1) * local] = lines_ref[:, block * BLOCK : (block + 1) * BLOCK]
    rows = shares_ref[...]
    way = lax.broadcasted_iota(jnp.int32, rows.shape, 1) // step - lax.broadcasted_iota(jnp.int32, rows.shape, 0) % local
    sorted_rows = rows
    for d in range(1 - local, local):
        if d:
            moved = pltpu.roll(pltpu.roll(rows, -d % owners, 0), d * step % BLOCK, 1)
            sorted_rows = jnp.where(way == d, moved, sorted_rows)
    shares_ref[...] = sorted_rows


def sums_kernel(quarters, dp_count, place_ref, *refs):
    ab_in, r_in, refs = refs[: quarters + 1], refs[quarters + 1 : 2 * quarters + 1], refs[2 * quarters + 1 :]
    outs, refs = refs[:quarters], refs[quarters:]
    causal_ref, anti_ref, a_ref, data_ref, done_ref, taps_ref = refs
    gather(quarters, place_ref, ab_in, r_in, a_ref, data_ref)
    tails = ab_in[:quarters] + r_in
    half, quarter = place_ref[0], place_ref[1]
    local = causal_ref.shape[0]

    def work(a_part, a_band, b_part, b_band):
        for g in range(local):
            lanes = slice(g * BLOCK, (g + 1) * BLOCK)
            for rows, sums in (
                (slice(0, BLOCK), a_part(a_band.at[g], rows_of(a_ref, lanes))),
                (slice(BLOCK, WIDE), b_part(b_band.at[g], rows_of(data_ref, lanes))),
            ):
                for p in range(2):
                    done_ref[2 * p : 2 * p + 2, g, rows] = sums[p].reshape(2, BLOCK, BLOCK).astype(jnp.bfloat16)

    @pl.when(half == 0)
    def lower():
        bands(quarters, dp_count, place_ref, tails, taps_ref, causal_ref, anti_ref, K // 2, K)
        work(causal_part, causal_ref, anti_part, anti_ref)

    @pl.when(half != 0)
    def upper():
        bands(quarters, dp_count, place_ref, tails, taps_ref, causal_ref, anti_ref, 0, K // 2)
        work(anti_part, anti_ref, causal_part, causal_ref)

    for j in range(quarters):
        outs[j][...] = done_ref[quarter ^ j].reshape(local * WIDE, BLOCK)


def owned_kernel(scale, place_ref, arrived_ref, out_ref):
    groups, rows = out_ref.shape
    local = BLOCK // rows
    quarters = groups // local
    total = arrived_ref[:quarters]
    for i in range(1, arrived_ref.shape[0] // quarters):
        total = total + arrived_ref[i * quarters : (i + 1) * quarters]
    total = total * scale
    for g in range(local):
        part = (total if g == 0 else pltpu.roll(total, BLOCK - g * rows, 1))[:, :rows]
        for q in range(quarters):
            out_ref[q * local + g : q * local + g + 1] = part[q : q + 1]


def outputs_kernel(js, place_ref, *refs):
    f32, bf16 = jnp.float32, jnp.bfloat16
    count = len(js)
    back, inputs = refs[:count], refs[count : count + 4]
    outputs, results, sem = refs[-9:-5], refs[-5:-1], refs[-1]
    half, quarter = place_ref[0], place_ref[1]
    width = results[0].shape[2]

    def copies(i):
        columns = pl.ds(pl.multiple_of((quarter ^ js[i]) * width, width), width)
        return [
            pltpu.make_async_copy(store.at[i], target.at[0, :, columns], sem.at[i, k])
            for k, (store, target) in enumerate(zip(results, outputs))
        ]

    for i in range(count):
        for g in range(width // BLOCK):
            lanes = slice(g * BLOCK, (g + 1) * BLOCK)
            columns = pl.ds(pl.multiple_of((quarter ^ js[i]) * width + g * BLOCK, BLOCK), BLOCK)
            pre, post, values, cot = [source[0, :, columns].astype(f32) for source in inputs]
            sums = back[i][g * WIDE : (g + 1) * WIDE].astype(f32)
            a_sum, b_sum = sums[:BLOCK], sums[BLOCK:]
            convolved, carried = jnp.where(half == 0, a_sum, b_sum), jnp.where(half == 0, b_sum, a_sum)
            for result, value in zip(results, (post * convolved, carried * values, cot * convolved, carried * pre)):
                result[i, :, lanes] = value.astype(bf16)
        for copy in copies(i):
            copy.start()
    for i in range(count):
        for copy in copies(i):
            copy.wait()


def gate_outputs(js, place, back, gates, earlier=()):
    hbm = [pl.BlockSpec(memory_space=pltpu.HBM)] * 4
    store = pltpu.VMEM((len(js), BLOCK, back[0].shape[0] // 2), jnp.bfloat16)
    return pl.pallas_call(
        lambda *refs: outputs_kernel(js, *refs),
        in_specs=[pl.BlockSpec(memory_space=pltpu.SMEM)] + vmem_specs(len(js) + 4) + hbm[: len(earlier)],
        out_specs=hbm,
        out_shape=[jax.ShapeDtypeStruct(gates[0].shape, jnp.bfloat16)] * 4,
        input_output_aliases={1 + len(js) + 4 + k: k for k in range(len(earlier))},
        scratch_shapes=[store] * 4 + [pltpu.SemaphoreType.DMA((len(js), 4))],
        compiler_params=pltpu.CompilerParams(vmem_limit_bytes=20 * 1024 * 1024),
        cost_estimate=pl.CostEstimate(flops=1000, bytes_accessed=1000, transcendentals=0),
        name="outputs",
    )(place, *[back[j] for j in js], *gates, *earlier)


def swapped(pre_gate, post_gate, values, cotangent, filters):
    parts, dp_count = lax.axis_size("seq"), lax.axis_size("dp")
    quarters = parts // 2
    channels, groups = pre_gate.shape[2], filters.shape[1]
    width, local = channels // quarters, groups // quarters
    seq_index = lax.axis_index("seq")
    place = jnp.stack([seq_index // quarters, seq_index % quarters, lax.axis_index("dp")]).astype(jnp.int32)
    owners = parts * dp_count
    rows = filters.shape[0]
    f32, bf16 = jnp.float32, jnp.bfloat16
    every = ("dp", "seq")

    taps = filters.T
    pieces = [taps]
    for p in range(1, dp_count):
        pieces.append(lax.ppermute(taps, "dp", [(i, i ^ p) for i in range(dp_count)]))

    gates = [pre_gate, post_gate, values, cotangent]
    lower = seq_index < quarters
    mixed = (pre_gate[0].astype(f32) * values[0]).astype(bf16)
    gated = (cotangent[0].astype(f32) * post_gate[0]).astype(bf16)
    a, b = jnp.where(lower, mixed, gated), jnp.where(lower, gated, mixed)
    store = pltpu.VMEM((quarters, BLOCK, width), bf16)
    short = jax.ShapeDtypeStruct((local * BLOCK + TAIL, BLOCK), bf16)
    message = jax.ShapeDtypeStruct((2 * local * BLOCK + TAIL, BLOCK), bf16)
    chunks = call(
        lambda *refs: pack_kernel(quarters, dp_count, *refs), "pack", place, pieces + [a, b],
        [short] * quarters + [short if j == SPLIT else message for j in range(quarters)], [pltpu.VMEM((quarters, local, BLOCK), f32)],
        flops=1000, nbytes=1000,
    )
    a_own, ab_own = chunks[:quarters], chunks[quarters:]
    r_in = [swap(a_own[j], quarters + j) for j in range(quarters)]
    ab_in = [ab_own[0]] + [swap(a_own[j] if j == SPLIT else ab_own[j], j) for j in range(1, quarters)]
    ab_in.append(swap(ab_own[SPLIT], SPLIT))

    band = pltpu.VMEM((local, 2 * BLOCK, K), bf16)
    store = pltpu.VMEM((quarters, BLOCK, width), bf16)
    whole = pltpu.VMEM((parts, BLOCK, width), bf16)
    done = pl.pallas_call(
        lambda *refs: sums_kernel(quarters, dp_count, *refs),
        in_specs=[pl.BlockSpec(memory_space=pltpu.SMEM)] + vmem_specs(2 * quarters + 1),
        out_specs=vmem_specs(quarters),
        out_shape=[jax.ShapeDtypeStruct((2 * local * BLOCK, BLOCK), bf16)] * quarters,
        scratch_shapes=[
            band, band, store, whole, pltpu.VMEM((quarters, local, WIDE, BLOCK), bf16),
            pltpu.VMEM((parts, 8, BLOCK), f32),
        ],
        compiler_params=pltpu.CompilerParams(vmem_limit_bytes=20 * 1024 * 1024),
        cost_estimate=pl.CostEstimate(flops=1000, bytes_accessed=1000, transcendentals=0),
        name="sums",
    )(place, *ab_in, *r_in)
    back = [done[0]] + [swap(done[j], j) for j in range(1, quarters)]
    token = lax.ppermute(done[0], "dp", [(i, i ^ 1) for i in range(dp_count)])
    (shares,) = call(
        lambda *refs: lags_kernel(quarters, *refs), "lags", place, ab_in + r_in,
        [jax.ShapeDtypeStruct((owners, BLOCK), f32)], [store, whole, pltpu.VMEM((local, K), f32)],
        flops=1000, nbytes=1000, after=[token],
    )
    arrived = lax.all_to_all(shares, every, 0, 0, tiled=True)

    early, last = [0, quarters - 1], list(range(1, quarters - 1))
    outputs = gate_outputs(early, place, back, gates)
    output, grad_pre, grad_post, grad_values = gate_outputs(last, place, back, gates, outputs)
    total_tokens = dp_count * parts * pre_gate.shape[1] * (channels // groups)
    (mine,) = call(
        lambda *refs: owned_kernel(1.0 / float(total_tokens**0.5), *refs), "owned", place, [arrived],
        [jax.ShapeDtypeStruct((groups, rows), f32)], flops=1000, nbytes=1000,
    )
    return output, grad_pre, grad_post, grad_values, mine.T


def solution(mesh):
    def chosen(*shard):
        fits = swap_fits(*shard)
        return (swapped if fits else shards)(*shard)

    return jax.shard_map(
        chosen,
        mesh=mesh,
        in_specs=(
            P("dp", "seq", None),
            P("dp", "seq", None),
            P("dp", "seq", None),
            P("dp", "seq", None),
            P(("dp", "seq"), None),
        ),
        out_specs=(
            P("dp", "seq", None),
            P("dp", "seq", None),
            P("dp", "seq", None),
            P("dp", "seq", None),
            P(("dp", "seq"), None),
        ),
        check_vma=False,
    )
```
